32 devices in a mesh: dp: 16 (over z, y, x), seq: 2 (over core).
Axes of the slice: x: 2, y: 2, z: 4, core: 2. Of those that a mesh axis runs over, the one named last changes fastest.
Arguments:
- hidden_in: bfloat16 [64, 512, 768], P('dp', 'seq'), may hold values from -6 to 6
- out_grad: bfloat16 [64, 512, 768], P('dp', 'seq')
- seg_lengths: int32 [64, 4], P('dp'), may hold values from 1 to 320, as said below
- attn_master: float32 [4, 768, 768], P(None, 'dp')
- ffn_master: float32 [2, 3072, 768], P(None, 'dp')
- attn_moment: float32 [4, 768, 768], P(None, 'dp')
- ffn_moment: float32 [2, 3072, 768], P(None, 'dp')
- gains: float32 [2, 768], replicated, may hold values from 0.2 to 4
- gain_first: float32 [2, 768], replicated
- gain_second: float32 [2, 768], replicated, as said below
- bias_table: float32 [32, 12], replicated, may hold values from -3 to 3
- bias_first: float32 [32, 12], replicated
- bias_second: float32 [32, 12], replicated, as said below
Outputs:
- hidden_out: bfloat16 [64, 512, 768], P('dp', 'seq')
- hidden_grad: float32 [64, 512, 768], P('dp', 'seq')
- new_attn: float32 [4, 768, 768], P('seq', 'dp')
- new_attn_moment: float32 [4, 768, 768], P(None, 'dp')
- new_ffn: float32 [2, 3072, 768], P('seq', 'dp')
- new_ffn_moment: float32 [2, 3072, 768], P(None, 'dp')
- new_gains: float32 [2, 768], replicated
- new_gain_first: float32 [2, 768], replicated
- new_gain_second: float32 [2, 768], replicated
- new_bias: float32 [32, 12], replicated
- new_bias_first: float32 [32, 12], replicated
- new_bias_second: float32 [32, 12], replicated
The draws below stay inside these ranges and needn't reach their ends.
Inputs may be any that keep to these rules, and one draw needn't show every extreme that they name: `seg_lengths`: each row has 4 segment lengths of at least 1 whose sum leaves fewer than 64 padding tokens at its end; one segment of each row, at a place drawn from the seed, has exactly 320 tokens. `gain_second`: Positive. `bias_second`: Positive.
All inputs are finite; a program needn't handle non-finite values.
Results may differ from the reference program's by a relative error of at most 0.012.
The reference program's roundings to bfloat16 on the way count: a program that leaves them out, or rounds other values in their place, can miss the bound.
Values may be sent and summed in bfloat16 or wider, within the bound.
No kernel may reach another device: no remote copies, remote signals or barrier semaphores. Data moves between devices by JAX's collectives and lax.ppermute only.
A program may use at most 256 MiB of HBM per device.

```python
import math
import jax
import jax.numpy as jnp
from jax import lax

D = 768
H = 12
DH = 64
FF = 3072
BUCKETS = 32
ROW_LEN = 512
SEGS = 4
ROWS_DEV = 4
NS_STEPS = 2
STEP = 10
ROWS = 64


def rising_scale(rows_total, rise):
    return jnp.exp(jnp.arange(rows_total, dtype=jnp.float32) * (math.log(rise) / max(rows_total - 1, 1)))


def moment_shape(key, noise, base, rise):
    keys = jax.random.split(key, 1)
    count, rows_total, cols_total = noise.shape
    col_scale = jnp.exp(jax.random.uniform(keys[0], (count, 1, cols_total), jnp.float32, 0.0, math.log(10.0)))
    row_scale = rising_scale(rows_total, rise)
    groups = max(ROWS // ROWS_DEV, 1)
    block_len = rows_total // groups
    heavy = jnp.where(jnp.arange(rows_total) >= rows_total - block_len, 7.0, 1.0).astype(jnp.float32)
    row_scale = (row_scale * heavy)[None, :, None]
    return base * row_scale * col_scale * noise / 12.0


def draw_out_grad(key, part):
    key = jax.random.fold_in(key, 3)
    keys = jax.random.split(key, 1)
    noise = jnp.clip(jax.random.normal(keys[0], (ROWS, ROW_LEN, D), jnp.float32), -5.0, 5.0)
    rise = 3.0
    row_scale = rising_scale(ROWS, rise) / math.sqrt(rise)
    pos_scale = rising_scale(ROW_LEN, rise) / math.sqrt(rise)
    return (noise * row_scale[:, None, None] * pos_scale[None, :, None]).astype(jnp.bfloat16)


def draw_seg_lengths(key, part):
    key = jax.random.fold_in(key, 11)
    keys = jax.random.split(key, 4)
    longest = ROW_LEN // 2 + ROW_LEN // 8
    padding = jax.random.randint(keys[0], (ROWS, 1), 0, ROW_LEN // 8)
    remain = ROW_LEN - longest - padding
    half_rest = remain // 2
    first_len = jax.random.randint(keys[1], (ROWS, 1), 1, half_rest)
    second_len = jax.random.randint(keys[2], (ROWS, 1), 1, half_rest)
    others = jnp.concatenate([first_len, second_len, remain - first_len - second_len], axis=1)
    place = jax.random.randint(keys[3], (ROWS, 1), 0, 4)
    index = jnp.arange(4, dtype=jnp.int32)[None, :]
    pick = jnp.clip(index - (index > place).astype(jnp.int32), 0, 2)
    chosen = jnp.take_along_axis(others, pick, axis=1)
    return jnp.where(index == place, longest, chosen).astype(jnp.int32)


def draw_attn_master(key, part):
    key = jax.random.fold_in(key, 21)
    scales = jnp.array([0.45, 0.45, 1.0, 8.0 ** 0.5], jnp.float32) * D ** (-0.5)
    noise = jnp.clip(jax.random.normal(key, (4, D, D), jnp.float32), -6.0, 6.0)
    return noise * scales[:, None, None]


def draw_ffn_master(key, part):
    key = jax.random.fold_in(key, 23)
    scales = jnp.array([D ** (-0.5), FF ** (-0.5)], jnp.float32)
    noise = jnp.clip(jax.random.normal(key, (2, FF, D), jnp.float32), -6.0, 6.0)
    return noise * scales[:, None, None]


def draw_attn_moment(key, part):
    key = jax.random.fold_in(key, 31)
    keys = jax.random.split(key, 2)
    base = (ROWS * ROW_LEN) ** 0.5
    noise = jnp.clip(jax.random.normal(keys[0], (4, D, D), jnp.float32), -5.0, 5.0)
    return moment_shape(keys[1], noise, base, 10.0)


def draw_ffn_moment(key, part):
    key = jax.random.fold_in(key, 33)
    keys = jax.random.split(key, 2)
    base = 0.5 * (ROWS * ROW_LEN) ** 0.5
    noise = jnp.clip(jax.random.normal(keys[0], (2, FF, D), jnp.float32), -5.0, 5.0)
    return moment_shape(keys[1], noise, base, 10.0)


def draw_gains(key, part):
    key = jax.random.fold_in(key, 41)
    factor = 1.0 + 0.1 * jnp.clip(jax.random.normal(key, (2, D), jnp.float32), -3.0, 3.0)
    return 0.6 * rising_scale(D, 3.0)[None, :] * factor


def first_draw(key, shape_in, base):
    noise = jnp.clip(jax.random.normal(key, shape_in, jnp.float32), -5.0, 5.0)
    return 0.11 * base * noise


def second_draw(key, shape_in, base):
    factor = jnp.exp(jax.random.uniform(key, shape_in, jnp.float32, 0.0, math.log(4.0)))
    return 0.001 * base * base * factor


def draw_gain_first(key, part):
    key = jax.random.fold_in(key, 51)
    return first_draw(key, (2, D), 2.0 * (ROWS * ROW_LEN) ** 0.5)


def draw_gain_second(key, part):
    key = jax.random.fold_in(key, 53)
    return second_draw(key, (2, D), 2.0 * (ROWS * ROW_LEN) ** 0.5)


def draw_bias_first(key, part):
    key = jax.random.fold_in(key, 55)
    return first_draw(key, (BUCKETS, H), (ROWS * ROW_LEN) ** 0.5)


def draw_bias_second(key, part):
    key = jax.random.fold_in(key, 57)
    return second_draw(key, (BUCKETS, H), (ROWS * ROW_LEN) ** 0.5)


def steps_of(rng, shape, cuts, smallest, top_value):
    def one(dim, blocks):
        draws = jax.random.uniform(jax.random.fold_in(jax.random.fold_in(rng, 6), dim), (blocks,), jnp.float32, smallest / len(cuts), top_value / len(cuts))
        return jnp.repeat(jnp.exp(draws), shape[dim] // blocks).reshape((-1,) + (1,) * (len(shape) - dim - 1))

    level = one(*cuts[0])
    for cut in cuts[1:]:
        level = level * one(*cut)
    return level


def gaussian(key, extent, spread, bound, cuts=(), kind=jnp.bfloat16):
    level = steps_of(key, extent, cuts, -0.22, 0.18) if cuts else 1.0
    drawn = jax.random.normal(key, extent, jnp.float32) * spread * level
    return jnp.minimum(jnp.maximum(drawn, -bound), bound).astype(kind)


def setup_inputs(seed: int = 0) -> dict:
    key_list = jax.random.split(jax.random.key(seed), 14)
    hidden_in = gaussian(key_list[0], (ROWS, ROW_LEN, D), 1.0, 6.0, ((0, 16), (1, 2)))
    out_grad = draw_out_grad(jax.random.fold_in(key_list[13], 71), 0)
    seg_lengths = draw_seg_lengths(jax.random.fold_in(key_list[13], 71), 0)
    attn_master = draw_attn_master(jax.random.fold_in(key_list[13], 71), 0)
    ffn_master = draw_ffn_master(jax.random.fold_in(key_list[13], 71), 0)
    attn_moment = draw_attn_moment(jax.random.fold_in(key_list[13], 71), 0)
    ffn_moment = draw_ffn_moment(jax.random.fold_in(key_list[13], 71), 0)
    gains = draw_gains(jax.random.fold_in(key_list[13], 71), 0)
    gain_first = draw_gain_first(jax.random.fold_in(key_list[13], 71), 0)
    gain_second = draw_gain_second(jax.random.fold_in(key_list[13], 71), 0)
    bias_table = gaussian(key_list[10], (BUCKETS, H), 0.5, 3.0, (), jnp.float32)
    bias_first = draw_bias_first(jax.random.fold_in(key_list[13], 71), 0)
    bias_second = draw_bias_second(jax.random.fold_in(key_list[13], 71), 0)
    return {"hidden_in": hidden_in, "out_grad": out_grad, "seg_lengths": seg_lengths, "attn_master": attn_master, "ffn_master": ffn_master, "attn_moment": attn_moment, "ffn_moment": ffn_moment, "gains": gains, "gain_first": gain_first, "gain_second": gain_second, "bias_table": bias_table, "bias_first": bias_first, "bias_second": bias_second}


@jax.custom_vjp
def low(v):
    return lax.optimization_barrier(v.astype(jnp.bfloat16)).astype(jnp.float32)

@jax.custom_vjp
def low_back(v):
    return v

def low_keep(v):
    return (low(v), None)

def low_pass(kept, grad):
    return (grad,)

def back_keep(v):
    return (v, None)

def back_low(kept, grad):
    return (low(grad),)
low.defvjp(low_keep, low_pass)
low_back.defvjp(back_keep, back_low)
bucket_edges = (1, 2, 3, 4, 5, 6, 7, 8, 12, 16, 23, 32, 46, 64, 91)
norm_eps = 1e-06
masked_score = -1000000000.0
coeff_a = 3.4445
coeff_b = -4.775
coeff_c = 2.0315
frob_eps = 1e-07
muon_beta = 0.95
muon_rate = 0.6
muon_decay = 0.01
adam_one = 0.9
adam_two = 0.999
adam_rate = 0.3
adam_eps = 1e-08

def exact_dot(left, right, form):
    return jnp.einsum(form, left, right, precision=lax.Precision.HIGHEST)

def bucket_of(query_pos, key_pos):
    offset = key_pos[None, :] - query_pos[:, None]
    distance = jnp.abs(offset)
    bucket = jnp.where(offset > 0, 16, 0).astype(jnp.int32)
    for edge_value in bucket_edges:
        bucket = bucket + (distance >= edge_value).astype(jnp.int32)
    return bucket

def rms_norm(value, gain):
    scale = lax.rsqrt(lax.optimization_barrier(jnp.mean(value * value, axis=-1, keepdims=True)) + norm_eps)
    return value * scale * gain

def segment_ids(seg_lengths):
    seg_ends = jnp.cumsum(seg_lengths, axis=-1)
    places = jnp.arange(ROW_LEN, dtype=jnp.int32)
    return lax.optimization_barrier(jnp.sum((places[None, :, None] >= seg_ends[:, None, :]).astype(jnp.int32), axis=-1))

def forward(hidden, attn_w, ffn_w, gains, table, seg_ids):
    row_count = hidden.shape[0]
    attn_low = low(attn_w)
    ffn_low = low(ffn_w)
    normed = low(rms_norm(hidden, gains[0]))
    projected = low_back(low(exact_dot(normed, attn_low[:3], 'rtd,cde->rtce')))
    places = jnp.arange(ROW_LEN, dtype=jnp.int32)
    onehot = (bucket_of(places, places)[:, :, None] == jnp.arange(BUCKETS, dtype=jnp.int32)).astype(jnp.float32)
    bias_map = exact_dot(onehot, table, 'qkb,bh->hqk')
    block_rows = math.gcd(row_count, max(1, 4096 // ROW_LEN))
    shaped = projected.reshape(row_count // block_rows, block_rows, ROW_LEN, 3, H, DH)
    seg_blocks = seg_ids.reshape(row_count // block_rows, block_rows, ROW_LEN)

    def attend(block_in):
        piece, seg_block = block_in
        queries = piece[:, :, 0]
        keys_in = piece[:, :, 1]
        values_in = piece[:, :, 2]
        scores = low_back(exact_dot(queries, keys_in, 'rqhe,rkhe->rhqk') + bias_map[None])
        same_seg = seg_block[:, None, :, None] == seg_block[:, None, None, :]
        scores = jnp.where(same_seg, scores, masked_score)
        row_max = lax.optimization_barrier(jnp.max(scores, axis=-1, keepdims=True))
        exp_scores = jnp.exp(scores - row_max)
        attn_probs = exp_scores / lax.optimization_barrier(jnp.sum(exp_scores, axis=-1, keepdims=True))
        return exact_dot(low(attn_probs), values_in, 'rhqk,rkhe->rqhe')
    context = lax.map(jax.checkpoint(attend), (shaped, seg_blocks))
    context = low_back(low(context.reshape(row_count, ROW_LEN, H * DH)))
    attn_out = low_back(exact_dot(context, attn_low[3], 'rtd,de->rte'))
    middle = hidden + attn_out
    normed_two = low(rms_norm(middle, gains[1]))
    pre_act = low_back(exact_dot(normed_two, ffn_low[0], 'rtd,fd->rtf'))
    activation = low(jax.nn.gelu(pre_act))
    return middle + exact_dot(activation, ffn_low[1], 'rtf,fd->rtd')

def muon(master, moment, grad, scale):
    moment = muon_beta * moment + grad
    frob = jnp.sqrt(lax.optimization_barrier(jnp.sum(moment * moment, axis=(1, 2), keepdims=True)))
    ortho = moment / (frob + frob_eps)
    for ns_turn in range(NS_STEPS):
        gram = exact_dot(ortho, ortho, 'mrd,mre->mde')
        poly = coeff_b * gram + coeff_c * exact_dot(gram, gram, 'mde,mef->mdf')
        ortho = coeff_a * ortho + exact_dot(ortho, poly, 'mrd,mde->mre')
    return (master * (1.0 - muon_rate * muon_decay) - muon_rate * scale * ortho, moment)

def adamw(param, first_in, second_in, grad):
    first_new = adam_one * first_in + (1.0 - adam_one) * grad
    second_new = adam_two * second_in + (1.0 - adam_two) * grad * grad
    fix_one = 1.0 - adam_one ** STEP
    fix_two = 1.0 - adam_two ** STEP
    update = first_new / fix_one / (jnp.sqrt(second_new / fix_two) + adam_eps)
    return (param - adam_rate * update, first_new, second_new)

def reference(hidden_in, out_grad, seg_lengths, attn_master, ffn_master, attn_moment, ffn_moment, gains, gain_first, gain_second, bias_table, bias_first, bias_second):
    seg_ids = segment_ids(seg_lengths)
    valid_mask = (seg_ids < SEGS).astype(jnp.float32)
    hidden = hidden_in.astype(jnp.float32)

    def bound_forward(hidden_arg, attn_arg, ffn_arg, gain_arg, table_arg):
        return forward(hidden_arg, attn_arg, ffn_arg, gain_arg, table_arg, seg_ids)
    output, pullback = jax.vjp(bound_forward, hidden, attn_master, ffn_master, gains, bias_table)
    cotangent = out_grad.astype(jnp.float32) * valid_mask[:, :, None]
    hidden_grad, attn_grad, ffn_grad, gain_grad, bias_grad = pullback(cotangent)
    new_attn, new_attn_moment = muon(attn_master, attn_moment, attn_grad, 1.0)
    new_ffn, new_ffn_moment = muon(ffn_master, ffn_moment, ffn_grad, math.sqrt(max(1.0, FF / D)))
    new_gains, new_gain_first, new_gain_second = adamw(gains, gain_first, gain_second, gain_grad)
    new_bias, new_bias_first, new_bias_second = adamw(bias_table, bias_first, bias_second, bias_grad)
    return (output.astype(jnp.bfloat16), hidden_grad, new_attn, new_attn_moment, new_ffn, new_ffn_moment, new_gains, new_gain_first, new_gain_second, new_bias, new_bias_first, new_bias_second)
```

```python
import functools
import math

import jax
import jax.numpy as jnp
import numpy as np
from jax import lax
from jax.experimental import pallas as pl
from jax.experimental.pallas import tpu as pltpu
from jax.sharding import PartitionSpec as P

D = 768
FF = 3072
NS_STEPS = 2
STEP = 10
TILE = 128

bucket_edges = (1, 2, 3, 4, 5, 6, 7, 8, 12, 16, 23, 32, 46, 64, 91)
norm_eps = 1e-06
masked_score = -1000000000.0
coeff_a = 3.4445
coeff_b = -4.775
coeff_c = 2.0315
frob_eps = 1e-07
muon_beta = 0.95
muon_rate = 0.6
muon_decay = 0.01
adam_one = 0.9
adam_two = 0.999
adam_rate = 0.3
adam_eps = 1e-08

BF = jnp.bfloat16
F32 = jnp.float32
NT = (((1,), (1,)), ((), ()))
NN = (((1,), (0,)), ((), ()))
TN = (((0,), (0,)), ((), ()))
SMALL = pl.CostEstimate(flops=1000, bytes_accessed=1000, transcendentals=0)


def mm(left, right, dims):
    return lax.dot_general(left, right, dims, preferred_element_type=F32)


def hbm(*values):
    return tuple(pltpu.with_memory_space_constraint(v, pltpu.HBM) for v in values)


def exact_dot(left, right, form):
    return jnp.einsum(form, left, right, precision=lax.Precision.HIGHEST)


def offset_onehot(buckets):
    offset = np.arange(4 * TILE) - (2 * TILE - 1)
    bucket = np.where(offset > 0, 16, 0)
    for edge_value in bucket_edges:
        bucket = bucket + (np.abs(offset) >= edge_value)
    hot = (bucket[:, None] == np.arange(buckets)).astype(np.float32)
    hot[-1] = 0.0
    return hot


def norm_back(scaled_grad, unit, scale):
    return scale * (scaled_grad - unit * jnp.mean(scaled_grad * unit, axis=-1, keepdims=True))


def adamw(param, first_in, second_in, grad):
    first_new = adam_one * first_in + (1.0 - adam_one) * grad
    second_new = adam_two * second_in + (1.0 - adam_two) * grad * grad
    fix_one = 1.0 - adam_one**STEP
    fix_two = 1.0 - adam_two**STEP
    update = first_new / fix_one / (jnp.sqrt(second_new / fix_two) + adam_eps)
    return (param - adam_rate * update, first_new, second_new)


def skew_tile(vector):
    width = vector.shape[1]
    base = pltpu.roll(jnp.broadcast_to(vector, (8, width)), width - (TILE - 1), axis=1)
    row = lax.broadcasted_iota(jnp.int32, (8, width), 0)
    head = base
    for i in range(1, 8):
        head = jnp.where(row == i, pltpu.roll(base, i, axis=1), head)
    pieces = [head] + [pltpu.roll(head, 8 * g, axis=1) for g in range(1, TILE // 8)]
    return jnp.concatenate(pieces, axis=0)


def unskew_sum(tile):
    width = tile.shape[1]
    rows = tile.shape[0]
    while rows > 8:
        half = rows // 2
        tile = tile[:half] + pltpu.roll(tile[half:], width - half, axis=1)
        rows = half
    row = lax.broadcasted_iota(jnp.int32, (8, width), 0)
    total = jnp.where(row == 0, tile, 0.0)
    for i in range(1, 8):
        total = total + jnp.where(row == i, pltpu.roll(tile, width - i, axis=1), 0.0)
    return pltpu.roll(jnp.broadcast_to(jnp.sum(total, axis=0, keepdims=True), (8, width)), TILE - 1, axis=1)[
        0:1
    ]


def bias_column(bias_ref, far, a, first_block, count, blocks):
    columns = []
    for qb in range(first_block, first_block + count):
        pieces = []
        for kb in range(blocks):
            diff = qb - kb
            if diff <= -2:
                pieces.append(far[a][0])
            elif diff >= 2:
                pieces.append(far[a][1])
            else:
                pieces.append(bias_ref[a, :, (diff + 1) * TILE : (diff + 2) * TILE])
        columns.append(jnp.concatenate(pieces, axis=0))
    return jnp.concatenate(columns, axis=1)


def bias_setup(trev_ref, bias_ref):
    far = []
    for a in range(2):
        vector = trev_ref[0, a : a + 1, :]
        bias_ref[a] = skew_tile(vector)
        far.append(
            (
                jnp.broadcast_to(vector[:, 0:1], (TILE, TILE)),
                jnp.broadcast_to(vector[:, 4 * TILE - 2 : 4 * TILE - 1], (TILE, TILE)),
            )
        )
    return far


def attend_kernel(
    rows, length, wide, extra, trev_ref, segk_ref, segq_ref, q_ref, k_ref, v_ref, *refs
):
    ctx_ref, lse_ref, bias_ref = refs[extra:]
    blocks = length // TILE
    lane = lax.broadcasted_iota(jnp.int32, (wide, TILE), 1)
    low_half = lane < TILE // 2
    far = bias_setup(trev_ref, bias_ref)
    for r in range(rows):
        span = slice(r * length, (r + 1) * length)
        keys = k_ref[0, span, :]
        values = v_ref[0, span, :]
        seg_k = segk_ref[r]
        for qt in range(length // wide):
            at = slice(r * length + qt * wide, r * length + (qt + 1) * wide)
            query = q_ref[0, at, :]
            same = seg_k == segq_ref[r, :, qt * wide : (qt + 1) * wide]
            outs = []
            for a in range(2):
                mine = low_half if a == 0 else jnp.logical_not(low_half)
                raw = mm(keys, jnp.where(mine, query, jnp.zeros_like(query)), NT)
                step = wide // TILE
                raw = raw + bias_column(bias_ref, far, a, qt * step, step, blocks)
                scores = jnp.where(same, raw, masked_score)
                row_max = jnp.max(scores, axis=0, keepdims=True)
                exp_scores = jnp.exp(scores - row_max)
                total = jnp.sum(exp_scores, axis=0, keepdims=True)
                probs = (exp_scores * (1.0 / total)).astype(BF)
                outs.append(mm(probs, values, TN))
                lse_ref[0, a : a + 1, at] = row_max + jnp.log(total)
            ctx_ref[at, :] = jnp.where(low_half, outs[0], outs[1]).astype(BF)


def attend(proj, trev, seg_col, seg_row, rows, length, first_pair, after=()):
    tokens = proj.shape[1]
    pairs = proj.shape[2] // TILE
    whole = lambda shape: pl.BlockSpec(shape, lambda p: (0,) * len(shape))
    part = lambda c: pl.BlockSpec((1, tokens, TILE), lambda p: (c, 0, p))
    return pl.pallas_call(
        functools.partial(attend_kernel, rows, length, 2 * TILE, len(after)),
        grid=(pairs,),
        in_specs=[
            pl.BlockSpec((1, 2, 4 * TILE), lambda p: (p + first_pair, 0, 0)),
            whole((rows, length, 1)),
            whole((rows, 1, length)),
            part(0),
            part(1),
            part(2),
        ]
        + [pl.BlockSpec(memory_space=pl.ANY)] * len(after),
        out_specs=[
            pl.BlockSpec((tokens, TILE), lambda p: (0, p)),
            pl.BlockSpec((1, 2, tokens), lambda p: (p, 0, 0)),
        ],
        out_shape=[
            jax.ShapeDtypeStruct((tokens, pairs * TILE), BF),
            jax.ShapeDtypeStruct((pairs, 2, tokens), F32),
        ],
        scratch_shapes=[pltpu.VMEM((2, TILE, 4 * TILE), F32)],
        compiler_params=pltpu.CompilerParams(vmem_limit_bytes=40 << 20),
        cost_estimate=SMALL,
        name="attend",
    )(trev, seg_col, seg_row, proj, proj, proj, *after)


def attend_back_kernel(
    rows,
    length,
    wide,
    extra,
    trev_ref,
    segk_ref,
    segq_ref,
    lse_ref,
    q_ref,
    k_ref,
    v_ref,
    do_ref,
    *refs,
):
    grad_ref, diag_ref, bias_ref, acc_ref = refs[extra:]
    blocks = length // TILE
    lane = lax.broadcasted_iota(jnp.int32, (wide, TILE), 1)
    low_half = lane < TILE // 2
    lane_row = lax.broadcasted_iota(jnp.int32, (1, 4 * TILE), 1)
    far = bias_setup(trev_ref, bias_ref)
    sums = [[jnp.zeros((8, TILE), F32) for _ in range(2)] for _ in range(2)]
    acc_ref[...] = jnp.zeros_like(acc_ref)
    step = wide // TILE
    for r in range(rows):
        span = slice(r * length, (r + 1) * length)
        keys = k_ref[0, span, :]
        values = v_ref[0, span, :]
        seg_k = segk_ref[r]
        key_grad = jnp.zeros((length, TILE), F32)
        value_grad = jnp.zeros((length, TILE), F32)
        for qt in range(length // wide):
            at = slice(r * length + qt * wide, r * length + (qt + 1) * wide)
            query = q_ref[0, at, :]
            do = do_ref[at, :]
            same = seg_k == segq_ref[r, :, qt * wide : (qt + 1) * wide]
            query_grads = []
            for a in range(2):
                mine = low_half if a == 0 else jnp.logical_not(low_half)
                query_a = jnp.where(mine, query, jnp.zeros_like(query))
                do_a = jnp.where(mine, do, jnp.zeros_like(do))
                raw = mm(keys, query_a, NT)
                raw = raw + bias_column(bias_ref, far, a, qt * step, step, blocks)
                scores = jnp.where(same, raw, masked_score)
                probs = jnp.exp(scores - lse_ref[0, a : a + 1, at])
                probs_grad = mm(values, do_a, NT)
                weighted = probs * probs_grad
                inner = jnp.sum(weighted, axis=0, keepdims=True)
                score_grad = (weighted - probs * inner).astype(BF)
                value_grad = value_grad + mm(probs.astype(BF), do_a, NN)
                key_grad = key_grad + mm(score_grad, query_a, NN)
                query_grads.append(mm(score_grad, keys, TN))
                for qs in range(step):
                    for kb in range(blocks):
                        diff = qt * step + qs - kb
                        piece = score_grad[
                            kb * TILE : (kb + 1) * TILE, qs * TILE : (qs + 1) * TILE
                        ].astype(F32)
                        if abs(diff) >= 2:
                            side = 0 if diff < 0 else 1
                            sums[a][side] = sums[a][side] + jnp.sum(
                                piece.reshape(TILE // 8, 8, TILE), axis=0
                            )
                        else:
                            acc_ref[a, :, (diff + 1) * TILE : (diff + 2) * TILE] += piece
            grad_ref[0, at, :] = jnp.where(low_half, query_grads[0], query_grads[1]).astype(BF)
        grad_ref[1, span, :] = key_grad.astype(BF)
        grad_ref[2, span, :] = value_grad.astype(BF)
    for a in range(2):
        near = unskew_sum(acc_ref[a])
        ends = [
            jnp.sum(jnp.sum(sums[a][side], axis=1, keepdims=True), axis=0, keepdims=True)
            for side in range(2)
        ]
        diag_ref[0, a : a + 1, :] = (
            near
            + jnp.where(lane_row == 0, ends[0], 0.0)
            + jnp.where(lane_row == 4 * TILE - 2, ends[1], 0.0)
        )


def attend_back(
    proj, trev, seg_col, seg_row, lse_rows, do, rows, length, pair, member, count, pairs, carried
):
    tokens = proj.shape[1]
    lanes = pairs * TILE
    whole = lambda shape: pl.BlockSpec(shape, lambda p: (0,) * len(shape))
    part = lambda c: pl.BlockSpec((1, tokens, TILE), lambda p: (c, 0, pair + p))
    one = lambda size, which: pl.BlockSpec((1, 2, size), lambda p: (which + p, 0, 0))
    extras = () if carried is None else (carried,)
    return pl.pallas_call(
        functools.partial(attend_back_kernel, rows, length, 2 * TILE, len(extras)),
        grid=(count,),
        in_specs=[
            one(4 * TILE, pair),
            whole((rows, length, 1)),
            whole((rows, 1, length)),
            one(tokens, pair),
            part(0),
            part(1),
            part(2),
            pl.BlockSpec((tokens, TILE), lambda p: (0, pair + p)),
        ]
        + [pl.BlockSpec(memory_space=pl.ANY)] * len(extras),
        out_specs=[
            pl.BlockSpec((3, tokens, TILE), lambda p: (0, 0, member + p)),
            one(4 * TILE, 0),
        ],
        out_shape=[
            jax.ShapeDtypeStruct((3, tokens, lanes), BF),
            jax.ShapeDtypeStruct((count, 2, 4 * TILE), F32),
        ],
        scratch_shapes=[
            pltpu.VMEM((2, TILE, 4 * TILE), F32),
            pltpu.VMEM((2, TILE, 4 * TILE), F32),
        ],
        input_output_aliases={} if carried is None else {8: 0},
        compiler_params=pltpu.CompilerParams(vmem_limit_bytes=48 << 20),
        cost_estimate=SMALL,
        name="attend_back",
    )(trev, seg_col, seg_row, lse_rows, *hbm(proj, proj, proj, do), *extras)


def ffn_kernel(extra, first_ref, normed_ref, cot_ref, w_ref, *refs):
    y_ref, dn_ref, keep_ref, send_ref = refs[extra:]
    step = pl.program_id(0)
    width = normed_ref.shape[1]

    @pl.when(step == 0)
    def _():
        y_ref[...] = jnp.zeros_like(y_ref)
        dn_ref[...] = jnp.zeros_like(dn_ref)

    w_in = w_ref[0].reshape(-1, width)
    w_out = w_ref[1].reshape(-1, width)
    normed = normed_ref[...]
    cot = cot_ref[...]
    pre = mm(w_in, normed, NT)
    act_grad = mm(w_out, cot, NT)
    square = pre * pre
    root = math.sqrt(2.0 / math.pi)
    tanh = jnp.tanh(pre * (root + (root * 0.044715) * square))
    half = 0.5 * (1.0 + tanh)
    act = (pre * half).astype(BF)
    slope = half + (0.5 * pre) * (1.0 - tanh * tanh) * (root + (3.0 * root * 0.044715) * square)
    pre_low = (act_grad * slope).astype(BF)
    y_ref[...] += mm(act, w_out, TN)
    dn_ref[...] += mm(pre_low, w_in, TN)
    down = mm(act, cot, NN)
    up = mm(pre_low, normed, NN)

    @pl.when(first_ref[0] == 1)
    def _():
        keep_ref[...] = up
        send_ref[...] = down.astype(BF)

    @pl.when(first_ref[0] == 0)
    def _():
        keep_ref[...] = down
        send_ref[...] = up.astype(BF)


def ffn(first, normed, cot, weights, places, part, after=()):
    tokens, width = normed.shape
    units = weights.shape[1] // 2
    half = units // places
    view = weights.reshape(2, places, 2, half, width)
    if half % 16 == 0:
        blocks = 384 // half
        chunk = blocks * half
        w_spec = pl.BlockSpec((2, blocks, None, half, width), lambda s: (0, s, part, 0, 0))
    else:
        chunk = 512
        view = view[:, :, part].reshape(2, units, width)
        w_spec = pl.BlockSpec((2, chunk, width), lambda s: (0, s, 0))
    whole = lambda shape, mode=None: pl.BlockSpec(
        shape, lambda s: (0,) * len(shape), pipeline_mode=mode
    )
    block = pl.BlockSpec((chunk, width), lambda s: (s, 0))
    once = pl.Buffered(1)
    return pl.pallas_call(
        functools.partial(ffn_kernel, len(after)),
        grid=(units // chunk,),
        in_specs=[
            pl.BlockSpec(memory_space=pltpu.SMEM),
            whole((tokens, width), once),
            whole((tokens, width), once),
            w_spec,
        ]
        + [pl.BlockSpec(memory_space=pl.ANY)] * len(after),
        out_specs=[whole((tokens, width)), whole((tokens, width)), block, block],
        out_shape=[
            jax.ShapeDtypeStruct((tokens, width), F32),
            jax.ShapeDtypeStruct((tokens, width), F32),
            jax.ShapeDtypeStruct((units, width), F32),
            jax.ShapeDtypeStruct((units, width), BF),
        ],
        compiler_params=pltpu.CompilerParams(vmem_limit_bytes=52 << 20),
        cost_estimate=SMALL,
        name="ffn",
    )(first, normed, cot, view, *after)


def token_maps(length):
    block = lambda r, far, core: 2 * r + jnp.bitwise_xor(core[0], far)
    return lambda r, far, core: (block(r, far, core), 0), lambda r, far, core: (r, 0, 0)


def middle_kernel(core_ref, middle_ref, cot_ref, gain_ref, out_w_ref, y0_ref, y1_ref, dn0_ref, dn1_ref, *refs):
    ctx_ref, own_ref, send_ref, grad_ref, ctx_grad_ref, map_grad_ref, gain_grad_ref = refs
    y_refs, dn_refs, ctx_refs = (y0_ref, y1_ref), (dn0_ref, dn1_ref), (ctx_ref,)
    middle = middle_ref[...]
    out = (middle + (y_refs[0][...] + y_refs[1][...])).astype(BF)

    @pl.when(pl.program_id(1) == 0)
    def _():
        own_ref[0] = out

    @pl.when(pl.program_id(1) == 1)
    def _():
        send_ref[0] = out

    dn = dn_refs[0][...] + dn_refs[1][...]
    scale = lax.rsqrt(jnp.mean(middle * middle, axis=1, keepdims=True) + norm_eps)
    unit = middle * scale
    scaled = dn * gain_ref[...]
    inner = jnp.mean(scaled * unit, axis=1, keepdims=True)
    grad = cot_ref[...].astype(F32) + scale * (scaled - unit * inner)
    grad_ref[...] = grad
    low = grad.astype(BF)
    ctx_grad_ref[...] = mm(low, out_w_ref[...], NT).astype(BF)
    map_grad = mm(ctx_refs[0][...], low, TN)
    gain_grad = jnp.sum((dn * unit).reshape(-1, 8, dn.shape[1]), axis=0)
    fresh = pl.program_id(0) + pl.program_id(1) == 0

    @pl.when(fresh)
    def _():
        map_grad_ref[...] = map_grad
        gain_grad_ref[...] = gain_grad

    @pl.when(jnp.logical_not(fresh))
    def _():
        map_grad_ref[...] += map_grad
        gain_grad_ref[...] += gain_grad


def middle_back(core, middle, cot, gain, out_w, y_parts, dn_parts, context, rows):
    tokens, width = middle.shape
    chunk = tokens // rows // 2
    here, row = token_maps(chunk)
    block = pl.BlockSpec((chunk, width), here)
    whole = lambda shape: pl.BlockSpec(shape, lambda r, far, core: (0,) * len(shape))
    half = pl.BlockSpec((1, chunk, width), row)
    return pl.pallas_call(
        middle_kernel,
        grid_spec=pltpu.PrefetchScalarGridSpec(
            num_scalar_prefetch=1,
            grid=(rows, 2),
            in_specs=[block, block, whole((1, width)), whole((width, width))] + [block] * 5,
            out_specs=[half, half, block, block, whole((width, width)), whole((8, width))],
        ),
        out_shape=[
            jax.ShapeDtypeStruct((rows, chunk, width), BF),
            jax.ShapeDtypeStruct((rows, chunk, width), BF),
            jax.ShapeDtypeStruct((tokens, width), F32),
            jax.ShapeDtypeStruct((tokens, width), BF),
            jax.ShapeDtypeStruct((width, width), F32),
            jax.ShapeDtypeStruct((8, width), F32),
        ],
        compiler_params=pltpu.CompilerParams(vmem_limit_bytes=40 << 20),
        cost_estimate=SMALL,
        name="middle_back",
    )(core, *hbm(middle, cot), gain, *hbm(out_w, *y_parts, *dn_parts, context))


def project_kernel(core_ref, normed_ref, own_ref, other_ref, out_ref):
    def each(w_ref):
        for c in range(3):
            out_ref[c] = mm(normed_ref[...], w_ref[c], NN).astype(BF)

    @pl.when(pl.program_id(0) == 0)
    def _():
        each(own_ref)

    @pl.when(pl.program_id(0) == 1)
    def _():
        each(other_ref)


def project(core, normed, own, other):
    tokens, width = normed.shape
    strip = own.shape[2]
    half = pl.BlockSpec((3, width, strip), lambda far, core: (0, 0, 0))
    return pl.pallas_call(
        project_kernel,
        grid_spec=pltpu.PrefetchScalarGridSpec(
            num_scalar_prefetch=1,
            grid=(2,),
            in_specs=[pl.BlockSpec((tokens, width), lambda far, core: (0, 0)), half, half],
            out_specs=pl.BlockSpec(
                (3, tokens, strip), lambda far, core: (0, 0, jnp.bitwise_xor(core[0], far))
            ),
        ),
        out_shape=jax.ShapeDtypeStruct((3, tokens, 2 * strip), BF),
        compiler_params=pltpu.CompilerParams(vmem_limit_bytes=40 << 20),
        cost_estimate=SMALL,
        name="project",
    )(core, normed, own, other)


def entry_kernel(core_ref, hidden_ref, grad_ref, gain_ref, w_own_ref, w_other_ref, *refs):
    grad_refs, (own_ref, send_ref, gain_grad_ref) = refs[:-3], refs[-3:]
    strip = w_own_ref.shape[2]

    def back(low, high):
        total = 0.0
        for c in range(3):
            grads = jnp.concatenate([ref[c] for ref in grad_refs], axis=1)
            total = total + mm(grads[:, :strip], low[c], NT) + mm(grads[:, strip:], high[c], NT)
        hidden = hidden_ref[...].astype(F32)
        scale = lax.rsqrt(jnp.mean(hidden * hidden, axis=1, keepdims=True) + norm_eps)
        unit = hidden * scale
        scaled = total * gain_ref[...]
        inner = jnp.mean(scaled * unit, axis=1, keepdims=True)
        result = grad_ref[...] + scale * (scaled - unit * inner)
        gain_grad = jnp.sum((total * unit).reshape(-1, 8, total.shape[1]), axis=0)
        far = pl.program_id(1)
        fresh = pl.program_id(0) + far == 0

        @pl.when(far == 0)
        def _():
            own_ref[0] = result

        @pl.when(far == 1)
        def _():
            send_ref[0] = result

        @pl.when(fresh)
        def _():
            gain_grad_ref[...] = gain_grad

        @pl.when(jnp.logical_not(fresh))
        def _():
            gain_grad_ref[...] += gain_grad

    @pl.when(core_ref[0] == 0)
    def _():
        back(w_own_ref, w_other_ref)

    @pl.when(core_ref[0] == 1)
    def _():
        back(w_other_ref, w_own_ref)


def entry_back(core, hidden, middle_grad, gain, own, other, grads, rows):
    tokens, width = hidden.shape
    chunk = tokens // rows // 2
    here, row = token_maps(chunk)
    block = pl.BlockSpec((chunk, width), here)
    whole = lambda shape: pl.BlockSpec(shape, lambda r, far, core: (0,) * len(shape))
    half = pl.BlockSpec((1, chunk, width), row)
    part = lambda lanes: pl.BlockSpec((3, chunk, lanes), lambda r, far, core: (0,) + here(r, far, core))
    return pl.pallas_call(
        entry_kernel,
        grid_spec=pltpu.PrefetchScalarGridSpec(
            num_scalar_prefetch=1,
            grid=(rows, 2),
            in_specs=[block, block, whole((1, width))]
            + [whole((3,) + own.shape[1:])] * 2
            + [part(v.shape[2]) for v in grads],
            out_specs=[half, half, whole((8, width))],
        ),
        out_shape=[
            jax.ShapeDtypeStruct((rows, chunk, width), F32),
            jax.ShapeDtypeStruct((rows, chunk, width), F32),
            jax.ShapeDtypeStruct((8, width), F32),
        ],
        compiler_params=pltpu.CompilerParams(vmem_limit_bytes=40 << 20),
        cost_estimate=SMALL,
        name="entry_back",
    )(core, *hbm(hidden, middle_grad), gain, *hbm(own, other, *grads))


def maps_kernel(first_ref, normed_ref, grads_ref, map_ref, *refs):
    keep_ref, send_ref = refs[-2:]
    normed = normed_ref[...]
    one, two, three = (mm(normed, grads_ref[c], TN) for c in range(3))
    four = map_ref[...]

    @pl.when(first_ref[0] == 1)
    def _():
        keep_ref[0], keep_ref[1] = one, two
        send_ref[0], send_ref[1] = three.astype(BF), four.astype(BF)

    @pl.when(first_ref[0] == 0)
    def _():
        keep_ref[0], keep_ref[1] = three, four
        send_ref[0], send_ref[1] = one.astype(BF), two.astype(BF)


def maps_grad(first, normed, grads, map_grad, start, after=()):
    tokens, width = normed.shape
    lanes = grads.shape[2]
    chunk = width // 3
    out = pl.BlockSpec((2, chunk, lanes), lambda s: (0, s, 0))
    return pl.pallas_call(
        maps_kernel,
        grid=(width // chunk,),
        in_specs=[
            pl.BlockSpec(memory_space=pltpu.SMEM),
            pl.BlockSpec((tokens, chunk), lambda s: (0, s)),
            pl.BlockSpec((3, tokens, lanes), lambda s: (0, 0, 0)),
            pl.BlockSpec((chunk, lanes), lambda s: (s, start // lanes)),
        ]
        + [pl.BlockSpec(memory_space=pl.ANY)] * len(after),
        out_specs=[out, out],
        out_shape=[
            jax.ShapeDtypeStruct((2, width, lanes), F32),
            jax.ShapeDtypeStruct((2, width, lanes), BF),
        ],
        compiler_params=pltpu.CompilerParams(vmem_limit_bytes=32 << 20),
        cost_estimate=SMALL,
        name="maps_grad",
    )(first, normed, grads, map_grad, *after)


FOLD = 2


def fold_kernel(order_ref, *refs):
    keep_out, send_out = refs[-2:]
    for j in range(FOLD):
        keep_ref, send_ref, got_keep_ref, got_send_ref = refs[4 * j : 4 * j + 4]
        keep_out[:, j : j + 1] = keep_ref[...] + got_keep_ref[...].astype(F32)
        send_out[:, j : j + 1] = (send_ref[...] + got_send_ref[...].astype(F32)).astype(BF)


def fold(value, got, order):
    many, count, rows, width = value.shape

    def at(which, j):
        return pl.BlockSpec(
            (many, 1, rows, width), lambda s, order: (0, order[which, FOLD * s + j], 0, 0)
        )

    out = pl.BlockSpec((many, FOLD, rows, width), lambda s, order: (0, s, 0, 0))
    shape = (many, count // 2, rows, width)
    return pl.pallas_call(
        fold_kernel,
        grid_spec=pltpu.PrefetchScalarGridSpec(
            num_scalar_prefetch=1,
            grid=(count // 2 // FOLD,),
            in_specs=[at(which, j) for j in range(FOLD) for which in (0, 1, 0, 1)],
            out_specs=[out, out],
        ),
        out_shape=[jax.ShapeDtypeStruct(shape, F32), jax.ShapeDtypeStruct(shape, BF)],
        compiler_params=pltpu.CompilerParams(vmem_limit_bytes=24 << 20),
        cost_estimate=SMALL,
        name="fold",
    )(order, *([value, value, got, got] * FOLD))


class Links:
    def __init__(self, clock):
        self.clock = clock
        self.size = lax.axis_size("dp")
        self.bits = self.size.bit_length() - 1
        self.place = lax.axis_index("dp")
        self.core = lax.axis_index("seq")
        self.first = self.core == 0

    def bit(self, number):
        return lax.rem(lax.div(self.place, 1 << number), 2)

    def turn_bit(self, turn):
        if turn > 1:
            return self.bit(turn)
        return jnp.where(self.first, self.bit(turn), self.bit(1 - turn))

    def swap_seq(self, value):
        return lax.ppermute(value, "seq", [(0, 1), (1, 0)])

    def swap_dp(self, value, turn):
        numbers = (turn, 1 - turn if turn <= 1 else turn)
        pairs = [
            (2 * i + c, 2 * (i ^ (1 << numbers[c])) + c) for i in range(self.size) for c in range(2)
        ]
        return lax.ppermute(value, ("dp", "seq"), pairs)

    def half_places(self):
        quads = np.arange(self.size // 4, dtype=np.int32)[:, None] * 4
        near = np.arange(2, dtype=np.int32)[None, :]
        bit = self.turn_bit(0)

        def places(wanted):
            return jnp.where(
                self.first, quads + near * 2 + wanted, quads + near + wanted * 2
            ).reshape(-1)

        return jnp.stack([places(bit), places(1 - bit)])


    def scatter_first(self, value, got):
        buf, send = fold(value, got, self.clock.after(self.places))
        came = yield send, functools.partial(self.swap_dp, turn=0)
        return buf + came.astype(F32)

    def scatter_rest(self, buf):
        many, _, rows, width = buf.shape
        for turn in range(1, self.bits):
            bit = self.turn_bit(turn)
            view = buf.reshape(many, -1, 2, rows, width)
            cut = lambda b: lax.dynamic_index_in_dim(view, b, 2, keepdims=False)
            send, buf = cut(1 - bit).astype(BF), cut(bit)
            came = yield send, functools.partial(self.swap_dp, turn=turn)
            buf = buf + came.astype(F32)
        return buf

    def scatter(self, value, got):
        buf = yield from self.scatter_first(value, got)
        return (yield from self.scatter_rest(buf))

    def sum_far(self, value):
        for turn in range(2, self.bits):
            low = value.astype(BF)
            came = yield low, functools.partial(self.swap_dp, turn=turn)
            value = low.astype(F32) + came.astype(F32)
        return value

    def order(self, bit, same, other, axis):
        return jnp.where(
            bit == 0, jnp.stack([same, other], axis=axis), jnp.stack([other, same], axis=axis)
        )

    def gather_near(self, buf, at):
        came = yield buf, functools.partial(self.swap_dp, turn=1)
        buf = self.order(self.turn_bit(1), buf, came, at)
        came = yield buf, functools.partial(self.swap_dp, turn=0)
        return jnp.where(
            self.first,
            self.order(self.bit(0), buf, came, at + 1),
            self.order(self.bit(1), buf, came, at),
        )

    def gather(self, value, axis):
        buf, at = value, axis
        for turn in range(self.bits - 1, 1, -1):
            came = yield buf, functools.partial(self.swap_dp, turn=turn)
            buf = self.order(self.bit(turn), buf, came, at)
            at += 1
        buf = yield from self.gather_near(buf, at)
        shape = value.shape
        return buf.reshape(shape[:axis] + (shape[axis] * self.size,) + shape[axis + 1 :])

    def sum_blocks(self, value):
        rows, width = value.shape
        view = value.reshape(2, 2, rows // 4, width)
        cut = lambda b: jnp.where(
            self.first,
            lax.dynamic_index_in_dim(view, b, 1, keepdims=False),
            lax.dynamic_index_in_dim(view, b, 0, keepdims=False),
        )
        bit = self.turn_bit(0)
        came = yield cut(1 - bit).astype(BF), functools.partial(self.swap_dp, turn=0)
        buf = cut(bit) + came.astype(F32)
        bit = self.turn_bit(1)
        half = lambda b: lax.dynamic_index_in_dim(buf, b, 0, keepdims=False)
        came = yield half(1 - bit).astype(BF), functools.partial(self.swap_dp, turn=1)
        buf = yield from self.sum_far(half(bit) + came.astype(F32))
        buf = yield from self.gather_near(buf.astype(BF), 0)
        return buf.reshape(rows, width)

    def all_sum(self, value):
        for turn in range(self.bits):
            came = yield value, functools.partial(self.swap_dp, turn=turn)
            value = value + came
        came = yield value, self.swap_seq
        return value + came

    def by_core(self, own, other, axis):
        return jnp.where(
            self.first,
            jnp.concatenate([own, other], axis=axis),
            jnp.concatenate([other, own], axis=axis),
        )


def tie(value, others):
    return lax.optimization_barrier((value, *others))[0]


class Order:
    def __init__(self):
        self.last = ()

    def after(self, value):
        return tie(value, self.last) if self.last else value

    def done(self, *values):
        self.last = values


class Chain:
    def __init__(self, order, steps):
        self.clock, self.steps, self.result = order, steps, None
        self.launch(*next(steps))

    def launch(self, send, how, free=False):
        self.flight, self.free = how(send), free
        self.clock.done(send)

    def step(self, count=1):
        for _ in range(count):
            if self.steps is None:
                return
            try:
                came = self.flight if self.free else self.clock.after(self.flight)
                self.launch(*self.steps.send(came))
            except StopIteration as end:
                self.result, self.steps = end.value, None
                self.clock.done(*jax.tree.leaves(self.result))

    def finish(self):
        while self.steps is not None:
            self.step()
        return self.result


def pack_gram(gram):
    count = gram.shape[0] // TILE
    row = lambda i: gram[i * TILE : (i + 1) * TILE, i * TILE :]
    return jnp.concatenate(
        [jnp.concatenate([row(i), row(count - 1 - i)], axis=1) for i in range(count // 2)], axis=0
    )


def unpack_gram(packed):
    count = 2 * packed.shape[0] // TILE
    blocks = {}
    for i in range(count // 2):
        strip = packed[i * TILE : (i + 1) * TILE]
        for j in range(i, count):
            blocks[i, j] = strip[:, (j - i) * TILE : (j - i + 1) * TILE]
        low = count - 1 - i
        for j in range(low, count):
            blocks[low, j] = strip[:, (count - i + j - low) * TILE : (count - i + j - low + 1) * TILE]
    rows = []
    for i in range(count):
        rows.append(
            jnp.concatenate([blocks[i, j] if j >= i else blocks[j, i].T for j in range(count)], axis=1)
        )
    return jnp.concatenate(rows, axis=0)


def muon_kernel(parts, gathered, scaling, *refs):
    sources, (mom_ref, master_ref, out_ref) = refs[:parts], refs[parts:]
    whole = jnp.concatenate([ref[0] for ref in sources], axis=1) if parts > 1 else sources[0][0]
    gram = mm(whole, whole, TN) if gathered else unpack_gram(whole.astype(F32))
    width = gram.shape[1]
    row = lax.broadcasted_iota(jnp.int32, (width, width), 0)
    column = lax.broadcasted_iota(jnp.int32, (width, width), 1)
    trace = jnp.sum(
        jnp.sum(jnp.where(row == column, gram, 0.0), axis=0, keepdims=True), axis=1, keepdims=True
    )
    scale = 1.0 / (jnp.sqrt(trace) + frob_eps)
    unit = gram * (scale * scale)
    unit_low = unit.astype(BF)
    rest_one = (coeff_b * unit + coeff_c * mm(unit_low, unit_low, NN)).astype(BF)
    cross = mm(rest_one, unit_low, NN)
    second = (
        (coeff_a * coeff_a) * unit
        + (2.0 * coeff_a) * cross
        + mm(rest_one, cross.astype(BF), NN)
    )
    second_low = second.astype(BF)
    rest_two = (coeff_b * second + coeff_c * mm(second_low, second_low, NN)).astype(BF)
    ortho = mom_ref[0] * scale
    ortho = coeff_a * ortho + mm(ortho.astype(BF), rest_one, NN)
    ortho = coeff_a * ortho + mm(ortho.astype(BF), rest_two, NN)
    out_ref[0] = master_ref[0] * (1.0 - muon_rate * muon_decay) - (muon_rate * scaling) * ortho


def gram_kernel(mom_ref, out_ref):
    low = mom_ref[...].astype(BF)
    out_ref[...] = pack_gram(mm(low, low, TN))


def packed_gram(mom):
    width = mom.shape[1]
    return pl.pallas_call(
        gram_kernel,
        out_shape=jax.ShapeDtypeStruct((width // 2, width + TILE), F32),
        compiler_params=pltpu.CompilerParams(vmem_limit_bytes=24 << 20),
        cost_estimate=SMALL,
        name="gram",
    )(mom)


def muon(sources, gathered, mom, master, scaling):
    count, rows, width = mom.shape
    one = lambda shape: pl.BlockSpec((1,) + shape, lambda m: (m, 0, 0))
    return pl.pallas_call(
        functools.partial(muon_kernel, len(sources), gathered, scaling),
        grid=(count,),
        in_specs=[one(v.shape[1:]) for v in sources] + [one((rows, width)), one((rows, width))],
        out_specs=one((rows, width)),
        out_shape=jax.ShapeDtypeStruct(mom.shape, F32),
        compiler_params=pltpu.CompilerParams(vmem_limit_bytes=48 << 20),
        cost_estimate=SMALL,
        name="muon",
    )(*sources, mom, master)


def per_device(
    hidden_in,
    out_grad,
    seg_lengths,
    attn_master,
    ffn_master,
    attn_moment,
    ffn_moment,
    gains,
    gain_first,
    gain_second,
    bias_table,
    bias_first,
    bias_second,
):
    clock = Order()
    links = Links(clock)
    row_len = hidden_in.shape[1] * lax.axis_size("seq")
    heads = bias_table.shape[1]
    core = links.core
    first = links.first
    flag = first.astype(jnp.int32).reshape(1)
    core_at = core.astype(jnp.int32).reshape(1)
    width = attn_master.shape[2]
    pairs = heads // 2
    strip = width // 2
    half = ffn_master.shape[1] // 2
    size = links.size

    def pick(value, count):
        return lax.dynamic_slice_in_dim(value, core * count, count, 0)

    ffn_own = lax.dynamic_slice_in_dim(ffn_master, core * half, half, axis=1).astype(BF)
    ffn_w = lax.all_gather(ffn_own, ("dp", "seq"), axis=1, tiled=True)

    def attn_weights(shard):
        own = yield from links.gather(shard, 1)
        other = yield own, links.swap_seq
        return own, other

    weights = Chain(
        clock,
        attn_weights(
            lax.dynamic_slice_in_dim(attn_master, core * strip, strip, axis=2).astype(BF)
        ),
    )

    def row_halves(value):
        view = value.reshape((2, value.shape[0] // 2) + value.shape[1:])
        own, send = (lax.dynamic_index_in_dim(view, c, 0, keepdims=False) for c in (core, 1 - core))
        return own, send

    hidden_own, hidden_send = row_halves(hidden_in)
    cot_own, cot_send = row_halves(out_grad)
    hidden_other = links.swap_seq(hidden_send)
    cot_other = links.swap_seq(cot_send)
    clock.done(hidden_send, cot_send)
    weights.step()

    rows = hidden_own.shape[0]
    tokens = rows * row_len
    hidden_low = links.by_core(hidden_own, clock.after(hidden_other), 1).reshape(tokens, width)
    hidden = hidden_low.astype(F32)
    scale_one = lax.rsqrt(jnp.mean(hidden * hidden, axis=-1, keepdims=True) + norm_eps)
    normed = (hidden * scale_one * gains[0]).astype(BF)
    clock.done(normed)
    weights.step()

    seg_rows = lax.dynamic_slice_in_dim(seg_lengths, core * rows, rows, 0)
    seg_ends = jnp.cumsum(seg_rows, axis=-1)
    places = jnp.arange(row_len, dtype=jnp.int32)
    seg_full = jnp.sum((places[None, :, None] >= seg_ends[:, None, :]).astype(jnp.int32), axis=-1)
    valid = (seg_full < seg_rows.shape[1]).reshape(tokens, 1)
    seg_col = seg_full.reshape(rows, row_len, 1)
    seg_row = seg_full.reshape(rows, 1, row_len)
    cot_rows = links.by_core(cot_own, clock.after(cot_other), 1).reshape(tokens, width)
    cotangent = jnp.where(valid, cot_rows, jnp.zeros((), BF))
    onehot = offset_onehot(bias_table.shape[0])
    onehot_rev = np.concatenate([onehot[-2::-1], onehot[-1:]], axis=0)
    trev = exact_dot(onehot_rev, bias_table, "mb,bh->hm").reshape(heads // 2, 2, 4 * TILE)
    links.places = links.half_places()
    clock.done(cotangent, seg_col, seg_row, trev, links.places)
    weights.step()

    moment_attn = pick(attn_moment, 2)
    w_own, w_other = weights.finish()
    proj = project(core_at, normed, w_own, w_other)
    out_w = links.by_core(w_own[3], w_other[3], 1)
    context, lse = attend(proj, trev, seg_col, seg_row, rows, row_len, 0)

    middle = hidden + mm(context, out_w, NN)
    scale_two = lax.rsqrt(jnp.mean(middle * middle, axis=-1, keepdims=True) + norm_eps)
    normed_two = (middle * scale_two * gains[1]).astype(BF)

    def ffn_first(keep, send):
        view = (1, size, half, width)
        came = yield send, links.swap_seq, True
        return (yield from links.scatter_first(keep.reshape(view), came.reshape(view)))

    def ffn_rest(first_part, second_part):
        buf = jnp.concatenate([first_part, second_part], axis=2)
        total = yield from links.scatter_rest(buf)
        return total.reshape(1, 2 * half, width)

    y_parts, dn_parts, sums = [], [], []
    clock.done(normed_two)
    for p in range(2):
        y, dn, keep, send = ffn(clock.after(flag), normed_two, cotangent, ffn_w, size, p)
        y_parts.append(y)
        dn_parts.append(dn)
        sums.append(Chain(clock, ffn_first(keep, send)))
    one, two = sums
    one.step()
    out_own, out_send, middle_grad, context_grad, out_map_grad, gain_two_part = middle_back(
        clock.after(core_at), middle, cotangent, gains[1:2], out_w, y_parts, dn_parts, context, rows
    )
    clock.done(gain_two_part)

    done_grads, diag = [], []
    near = [0, 0]
    sizes = (pairs - pairs // 3, pairs // 3)

    def back(group, grads, count=2):
        start, member = sum(sizes[:group]), near[group]
        near[group] += count
        grads, diag_m = attend_back(
            proj,
            trev,
            seg_col,
            clock.after(seg_row),
            lse,
            context_grad,
            rows,
            row_len,
            start + member,
            member,
            count,
            sizes[group],
            grads,
        )
        diag.append(diag_m)
        clock.done(diag_m)
        return grads

    def maps(group, grads):
        done_grads.append(grads)
        keep, send = maps_grad(
            clock.after(flag), normed, grads, out_map_grad, sum(sizes[:group]) * TILE
        )
        clock.done(send)
        return keep, send

    def attn_first(group, keep, send):
        view = (2, size, width // size, sizes[group] * TILE)
        came = yield send, links.swap_seq, True
        return (yield from links.scatter_first(keep.reshape(view), came.reshape(view)))

    def attn_rest(first_group, second_group):
        buf = jnp.concatenate([first_group, second_group], axis=3)
        total = yield from links.scatter_rest(buf)
        grad = total.reshape(2, width // size, width)
        mom = muon_beta * moment_attn + grad
        whole = yield from links.gather(mom.astype(BF), 1)
        return grad, mom, whole

    two.step()
    grads = back(0, None)
    grads = back(0, grads)
    first_part, second_part = one.finish(), two.finish()
    units = Chain(clock, ffn_rest(first_part, second_part))
    three = Chain(clock, attn_first(0, *maps(0, grads)))
    grads = back(1, None)
    three.step()
    four = Chain(clock, attn_first(1, *maps(1, grads)))
    units.step()
    four.step()
    grad_own, grad_send, gain_one_part = entry_back(
        clock.after(core_at), hidden_low, middle_grad, gains[0:1], w_own, w_other, done_grads, rows
    )
    clock.done(gain_one_part)
    first_group, second_group = three.finish(), four.finish()
    maps_sum = Chain(clock, attn_rest(first_group, second_group))
    units.step()
    out_other = links.swap_seq(clock.after(out_send))
    diag = jnp.concatenate(diag, axis=0).reshape(heads, 4 * TILE)
    table_grad = exact_dot(onehot_rev, diag, "mb,hm->bh")
    small = jnp.concatenate(
        [
            jnp.sum(gain_one_part, axis=0),
            jnp.sum(gain_two_part, axis=0),
            table_grad.reshape(-1),
        ]
    )
    small = Chain(clock, links.all_sum(small))
    maps_sum.step()
    ffn_grad = units.finish()
    mom_ffn = muon_beta * pick(ffn_moment, 1) + ffn_grad
    gram = Chain(clock, links.sum_blocks(packed_gram(mom_ffn[0])))
    hidden_out = links.by_core(out_own, clock.after(out_other), 0)
    clock.done(hidden_out)
    maps_sum.step()
    gram.step()
    small.step()
    grad_other = links.swap_seq(clock.after(grad_send))
    maps_sum.step()
    gram.step()
    small.step()
    grad_tokens = links.by_core(grad_own, clock.after(grad_other), 0)
    clock.done(grad_tokens)
    gram.step()
    maps_sum.step()
    ffn_other = links.swap_seq(clock.after(ffn_grad))
    small.step()
    gram.step()
    ffn_mom = muon_beta * ffn_moment + links.by_core(ffn_grad, clock.after(ffn_other), 0)
    clock.done(ffn_mom)
    maps_sum.step()
    gram.step()
    small.step()
    maps_sum.step()
    if links.bits > 4:
        maps_sum.step(2 * links.bits - 8)
    gram_ffn, small = gram.finish(), small.finish()
    gain_sum = small[: 2 * width].reshape(2, width)
    table_sum = small[2 * width :].reshape(table_grad.shape)
    new_ffn = muon(
        [gram_ffn[None]],
        False,
        clock.after(mom_ffn),
        pick(ffn_master, 1),
        math.sqrt(max(1.0, FF / D)),
    )
    clock.done(new_ffn)
    attn_grad, mom_attn, attn_whole = maps_sum.finish()
    attn_other = links.swap_seq(attn_grad)
    new_attn = muon([attn_whole], True, mom_attn, pick(attn_master, 2), 1.0)
    attn_mom = muon_beta * attn_moment + links.by_core(attn_grad, attn_other, 0)
    new_gains, new_gain_first, new_gain_second = adamw(gains, gain_first, gain_second, gain_sum)
    new_bias, new_bias_first, new_bias_second = adamw(
        bias_table, bias_first, bias_second, table_sum
    )
    return (
        hidden_out,
        grad_tokens,
        new_attn,
        attn_mom,
        new_ffn,
        ffn_mom,
        new_gains,
        new_gain_first,
        new_gain_second,
        new_bias,
        new_bias_first,
        new_bias_second,
    )


def solution(mesh):
    in_specs = (
        P("dp", "seq", None),
        P("dp", "seq", None),
        P("dp", None),
        P(None, "dp", None),
        P(None, "dp", None),
        P(None, "dp", None),
        P(None, "dp", None),
        P(),
        P(),
        P(),
        P(),
        P(),
        P(),
    )
    out_specs = (
        P("dp", "seq", None),
        P("dp", "seq", None),
        P("seq", "dp", None),
        P(None, "dp", None),
        P("seq", "dp", None),
        P(None, "dp", None),
        P(),
        P(),
        P(),
        P(),
        P(),
        P(),
    )
    return jax.shard_map(
        per_device, mesh=mesh, in_specs=in_specs, out_specs=out_specs, check_vma=False
    )
```

```python
import functools
import math

import jax
import jax.numpy as jnp
import numpy as np
from jax import lax
from jax.experimental import pallas as pl
from jax.experimental.pallas import tpu as pltpu
from jax.sharding import PartitionSpec as P

D = 768
FF = 3072
NS_STEPS = 2
STEP = 10
TILE = 128

bucket_edges = (1, 2, 3, 4, 5, 6, 7, 8, 12, 16, 23, 32, 46, 64, 91)
norm_eps = 1e-06
masked_score = -1000000000.0
coeff_a = 3.4445
coeff_b = -4.775
coeff_c = 2.0315
frob_eps = 1e-07
muon_beta = 0.95
muon_rate = 0.6
muon_decay = 0.01
adam_one = 0.9
adam_two = 0.999
adam_rate = 0.3
adam_eps = 1e-08

BF = jnp.bfloat16
F32 = jnp.float32
NT = (((1,), (1,)), ((), ()))
NN = (((1,), (0,)), ((), ()))
TN = (((0,), (0,)), ((), ()))
SMALL = pl.CostEstimate(flops=1000, bytes_accessed=1000, transcendentals=0)


def mm(left, right, dims):
    return lax.dot_general(left, right, dims, preferred_element_type=F32)


def hbm(*values):
    return tuple(pltpu.with_memory_space_constraint(v, pltpu.HBM) for v in values)


def exact_dot(left, right, form):
    return jnp.einsum(form, left, right, precision=lax.Precision.HIGHEST)


def offset_onehot(buckets):
    offset = np.arange(4 * TILE) - (2 * TILE - 1)
    bucket = np.where(offset > 0, 16, 0)
    for edge_value in bucket_edges:
        bucket = bucket + (np.abs(offset) >= edge_value)
    hot = (bucket[:, None] == np.arange(buckets)).astype(np.float32)
    hot[-1] = 0.0
    return hot


def norm_back(scaled_grad, unit, scale):
    return scale * (scaled_grad - unit * jnp.mean(scaled_grad * unit, axis=-1, keepdims=True))


def adamw(param, first_in, second_in, grad):
    first_new = adam_one * first_in + (1.0 - adam_one) * grad
    second_new = adam_two * second_in + (1.0 - adam_two) * grad * grad
    fix_one = 1.0 - adam_one**STEP
    fix_two = 1.0 - adam_two**STEP
    update = first_new / fix_one / (jnp.sqrt(second_new / fix_two) + adam_eps)
    return (param - adam_rate * update, first_new, second_new)


def skew_tile(vector):
    width = vector.shape[1]
    base = pltpu.roll(jnp.broadcast_to(vector, (8, width)), width - (TILE - 1), axis=1)
    row = lax.broadcasted_iota(jnp.int32, (8, width), 0)
    head = base
    for i in range(1, 8):
        head = jnp.where(row == i, pltpu.roll(base, i, axis=1), head)
    pieces = [head] + [pltpu.roll(head, 8 * g, axis=1) for g in range(1, TILE // 8)]
    return jnp.concatenate(pieces, axis=0)


def unskew_sum(tile):
    width = tile.shape[1]
    rows = tile.shape[0]
    while rows > 8:
        half = rows // 2
        tile = tile[:half] + pltpu.roll(tile[half:], width - half, axis=1)
        rows = half
    row = lax.broadcasted_iota(jnp.int32, (8, width), 0)
    total = jnp.where(row == 0, tile, 0.0)
    for i in range(1, 8):
        total = total + jnp.where(row == i, pltpu.roll(tile, width - i, axis=1), 0.0)
    return pltpu.roll(jnp.broadcast_to(jnp.sum(total, axis=0, keepdims=True), (8, width)), TILE - 1, axis=1)[
        0:1
    ]


def bias_column(bias_ref, far, a, first_block, count, blocks):
    columns = []
    for qb in range(first_block, first_block + count):
        pieces = []
        for kb in range(blocks):
            diff = qb - kb
            if diff <= -2:
                pieces.append(far[a][0])
            elif diff >= 2:
                pieces.append(far[a][1])
            else:
                pieces.append(bias_ref[a, :, (diff + 1) * TILE : (diff + 2) * TILE])
        columns.append(jnp.concatenate(pieces, axis=0))
    return jnp.concatenate(columns, axis=1)


def bias_setup(trev_ref, bias_ref):
    far = []
    for a in range(2):
        vector = trev_ref[0, a : a + 1, :]
        bias_ref[a] = skew_tile(vector)
        far.append(
            (
                jnp.broadcast_to(vector[:, 0:1], (TILE, TILE)),
                jnp.broadcast_to(vector[:, 4 * TILE - 2 : 4 * TILE - 1], (TILE, TILE)),
            )
        )
    return far


def attend_kernel(
    rows, length, wide, extra, trev_ref, segk_ref, segq_ref, q_ref, k_ref, v_ref, *refs
):
    ctx_ref, lse_ref, bias_ref = refs[extra:]
    blocks = length // TILE
    lane = lax.broadcasted_iota(jnp.int32, (wide, TILE), 1)
    low_half = lane < TILE // 2
    far = bias_setup(trev_ref, bias_ref)
    for r in range(rows):
        span = slice(r * length, (r + 1) * length)
        keys = k_ref[0, span, :]
        values = v_ref[0, span, :]
        seg_k = segk_ref[r]
        for qt in range(length // wide):
            at = slice(r * length + qt * wide, r * length + (qt + 1) * wide)
            query = q_ref[0, at, :]
            same = seg_k == segq_ref[r, :, qt * wide : (qt + 1) * wide]
            outs = []
            for a in range(2):
                mine = low_half if a == 0 else jnp.logical_not(low_half)
                raw = mm(keys, jnp.where(mine, query, jnp.zeros_like(query)), NT)
                step = wide // TILE
                raw = raw + bias_column(bias_ref, far, a, qt * step, step, blocks)
                scores = jnp.where(same, raw, masked_score)
                row_max = jnp.max(scores, axis=0, keepdims=True)
                exp_scores = jnp.exp(scores - row_max)
                total = jnp.sum(exp_scores, axis=0, keepdims=True)
                probs = (exp_scores * (1.0 / total)).astype(BF)
                outs.append(mm(probs, values, TN))
                lse_ref[0, a : a + 1, at] = row_max + jnp.log(total)
            ctx_ref[at, :] = jnp.where(low_half, outs[0], outs[1]).astype(BF)


def attend(proj, trev, seg_col, seg_row, rows, length, first_pair, after=()):
    tokens = proj.shape[1]
    pairs = proj.shape[2] // TILE
    whole = lambda shape: pl.BlockSpec(shape, lambda p: (0,) * len(shape))
    part = lambda c: pl.BlockSpec((1, tokens, TILE), lambda p: (c, 0, p))
    return pl.pallas_call(
        functools.partial(attend_kernel, rows, length, 2 * TILE, len(after)),
        grid=(pairs,),
        in_specs=[
            pl.BlockSpec((1, 2, 4 * TILE), lambda p: (p + first_pair, 0, 0)),
            whole((rows, length, 1)),
            whole((rows, 1, length)),
            part(0),
            part(1),
            part(2),
        ]
        + [pl.BlockSpec(memory_space=pl.ANY)] * len(after),
        out_specs=[
            pl.BlockSpec((tokens, TILE), lambda p: (0, p)),
            pl.BlockSpec((1, 2, tokens), lambda p: (p, 0, 0)),
        ],
        out_shape=[
            jax.ShapeDtypeStruct((tokens, pairs * TILE), BF),
            jax.ShapeDtypeStruct((pairs, 2, tokens), F32),
        ],
        scratch_shapes=[pltpu.VMEM((2, TILE, 4 * TILE), F32)],
        compiler_params=pltpu.CompilerParams(vmem_limit_bytes=40 << 20),
        cost_estimate=SMALL,
        name="attend",
    )(trev, seg_col, seg_row, proj, proj, proj, *after)


def attend_back_kernel(
    rows,
    length,
    wide,
    extra,
    trev_ref,
    segk_ref,
    segq_ref,
    lse_ref,
    q_ref,
    k_ref,
    v_ref,
    do_ref,
    *refs,
):
    grad_ref, diag_ref, bias_ref, acc_ref = refs[extra:]
    blocks = length // TILE
    lane = lax.broadcasted_iota(jnp.int32, (wide, TILE), 1)
    low_half = lane < TILE // 2
    lane_row = lax.broadcasted_iota(jnp.int32, (1, 4 * TILE), 1)
    far = bias_setup(trev_ref, bias_ref)
    sums = [[jnp.zeros((8, TILE), F32) for _ in range(2)] for _ in range(2)]
    acc_ref[...] = jnp.zeros_like(acc_ref)
    step = wide // TILE
    for r in range(rows):
        span = slice(r * length, (r + 1) * length)
        keys = k_ref[0, span, :]
        values = v_ref[0, span, :]
        seg_k = segk_ref[r]
        key_grad = jnp.zeros((length, TILE), F32)
        value_grad = jnp.zeros((length, TILE), F32)
        for qt in range(length // wide):
            at = slice(r * length + qt * wide, r * length + (qt + 1) * wide)
            query = q_ref[0, at, :]
            do = do_ref[at, :]
            same = seg_k == segq_ref[r, :, qt * wide : (qt + 1) * wide]
            query_grads = []
            for a in range(2):
                mine = low_half if a == 0 else jnp.logical_not(low_half)
                query_a = jnp.where(mine, query, jnp.zeros_like(query))
                do_a = jnp.where(mine, do, jnp.zeros_like(do))
                raw = mm(keys, query_a, NT)
                raw = raw + bias_column(bias_ref, far, a, qt * step, step, blocks)
                scores = jnp.where(same, raw, masked_score)
                probs = jnp.exp(scores - lse_ref[0, a : a + 1, at])
                probs_grad = mm(values, do_a, NT)
                weighted = probs * probs_grad
                inner = jnp.sum(weighted, axis=0, keepdims=True)
                score_grad = (weighted - probs * inner).astype(BF)
                value_grad = value_grad + mm(probs.astype(BF), do_a, NN)
                key_grad = key_grad + mm(score_grad, query_a, NN)
                query_grads.append(mm(score_grad, keys, TN))
                for qs in range(step):
                    for kb in range(blocks):
                        diff = qt * step + qs - kb
                        piece = score_grad[
                            kb * TILE : (kb + 1) * TILE, qs * TILE : (qs + 1) * TILE
                        ].astype(F32)
                        if abs(diff) >= 2:
                            side = 0 if diff < 0 else 1
                            sums[a][side] = sums[a][side] + jnp.sum(
                                piece.reshape(TILE // 8, 8, TILE), axis=0
                            )
                        else:
                            acc_ref[a, :, (diff + 1) * TILE : (diff + 2) * TILE] += piece
            grad_ref[0, at, :] = jnp.where(low_half, query_grads[0], query_grads[1]).astype(BF)
        grad_ref[1, span, :] = key_grad.astype(BF)
        grad_ref[2, span, :] = value_grad.astype(BF)
    for a in range(2):
        near = unskew_sum(acc_ref[a])
        ends = [
            jnp.sum(jnp.sum(sums[a][side], axis=1, keepdims=True), axis=0, keepdims=True)
            for side in range(2)
        ]
        diag_ref[0, a : a + 1, :] = (
            near
            + jnp.where(lane_row == 0, ends[0], 0.0)
            + jnp.where(lane_row == 4 * TILE - 2, ends[1], 0.0)
        )


def attend_back(
    proj, trev, seg_col, seg_row, lse_rows, do, rows, length, pair, member, count, pairs, carried
):
    tokens = proj.shape[1]
    lanes = pairs * TILE
    whole = lambda shape: pl.BlockSpec(shape, lambda p: (0,) * len(shape))
    part = lambda c: pl.BlockSpec((1, tokens, TILE), lambda p: (c, 0, pair + p))
    one = lambda size, which: pl.BlockSpec((1, 2, size), lambda p: (which + p, 0, 0))
    extras = () if carried is None else (carried,)
    return pl.pallas_call(
        functools.partial(attend_back_kernel, rows, length, 2 * TILE, len(extras)),
        grid=(count,),
        in_specs=[
            one(4 * TILE, pair),
            whole((rows, length, 1)),
            whole((rows, 1, length)),
            one(tokens, pair),
            part(0),
            part(1),
            part(2),
            pl.BlockSpec((tokens, TILE), lambda p: (0, pair + p)),
        ]
        + [pl.BlockSpec(memory_space=pl.ANY)] * len(extras),
        out_specs=[
            pl.BlockSpec((3, tokens, TILE), lambda p: (0, 0, member + p)),
            one(4 * TILE, 0),
        ],
        out_shape=[
            jax.ShapeDtypeStruct((3, tokens, lanes), BF),
            jax.ShapeDtypeStruct((count, 2, 4 * TILE), F32),
        ],
        scratch_shapes=[
            pltpu.VMEM((2, TILE, 4 * TILE), F32),
            pltpu.VMEM((2, TILE, 4 * TILE), F32),
        ],
        input_output_aliases={} if carried is None else {8: 0},
        compiler_params=pltpu.CompilerParams(vmem_limit_bytes=48 << 20),
        cost_estimate=SMALL,
        name="attend_back",
    )(trev, seg_col, seg_row, lse_rows, *hbm(proj, proj, proj, do), *extras)


def ffn_kernel(extra, first_ref, normed_ref, cot_ref, w_ref, *refs):
    y_ref, dn_ref, keep_ref, send_ref = refs[extra:]
    step = pl.program_id(0)
    width = normed_ref.shape[1]

    @pl.when(step == 0)
    def _():
        y_ref[...] = jnp.zeros_like(y_ref)
        dn_ref[...] = jnp.zeros_like(dn_ref)

    w_in = w_ref[0].reshape(-1, width)
    w_out = w_ref[1].reshape(-1, width)
    normed = normed_ref[...]
    cot = cot_ref[...]
    pre = mm(w_in, normed, NT)
    act_grad = mm(w_out, cot, NT)
    square = pre * pre
    root = math.sqrt(2.0 / math.pi)
    tanh = jnp.tanh(pre * (root + (root * 0.044715) * square))
    half = 0.5 * (1.0 + tanh)
    act = (pre * half).astype(BF)
    slope = half + (0.5 * pre) * (1.0 - tanh * tanh) * (root + (3.0 * root * 0.044715) * square)
    pre_low = (act_grad * slope).astype(BF)
    y_ref[...] += mm(act, w_out, TN)
    dn_ref[...] += mm(pre_low, w_in, TN)
    down = mm(act, cot, NN)
    up = mm(pre_low, normed, NN)

    @pl.when(first_ref[0] == 1)
    def _():
        keep_ref[...] = up
        send_ref[...] = down.astype(BF)

    @pl.when(first_ref[0] == 0)
    def _():
        keep_ref[...] = down
        send_ref[...] = up.astype(BF)


def ffn(first, normed, cot, weights, places, part, after=()):
    tokens, width = normed.shape
    units = weights.shape[1] // 2
    half = units // places
    view = weights.reshape(2, places, 2, half, width)
    if half % 16 == 0:
        blocks = 384 // half
        chunk = blocks * half
        w_spec = pl.BlockSpec((2, blocks, None, half, width), lambda s: (0, s, part, 0, 0))
    else:
        chunk = 512
        view = view[:, :, part].reshape(2, units, width)
        w_spec = pl.BlockSpec((2, chunk, width), lambda s: (0, s, 0))
    whole = lambda shape, mode=None: pl.BlockSpec(
        shape, lambda s: (0,) * len(shape), pipeline_mode=mode
    )
    block = pl.BlockSpec((chunk, width), lambda s: (s, 0))
    once = pl.Buffered(1)
    return pl.pallas_call(
        functools.partial(ffn_kernel, len(after)),
        grid=(units // chunk,),
        in_specs=[
            pl.BlockSpec(memory_space=pltpu.SMEM),
            whole((tokens, width), once),
            whole((tokens, width), once),
            w_spec,
        ]
        + [pl.BlockSpec(memory_space=pl.ANY)] * len(after),
        out_specs=[whole((tokens, width)), whole((tokens, width)), block, block],
        out_shape=[
            jax.ShapeDtypeStruct((tokens, width), F32),
            jax.ShapeDtypeStruct((tokens, width), F32),
            jax.ShapeDtypeStruct((units, width), F32),
            jax.ShapeDtypeStruct((units, width), BF),
        ],
        compiler_params=pltpu.CompilerParams(vmem_limit_bytes=52 << 20),
        cost_estimate=SMALL,
        name="ffn",
    )(first, normed, cot, view, *after)


def token_maps(length):
    block = lambda r, far, core: 2 * r + jnp.bitwise_xor(core[0], far)
    return lambda r, far, core: (block(r, far, core), 0), lambda r, far, core: (r, 0, 0)


def middle_kernel(core_ref, middle_ref, cot_ref, gain_ref, out_w_ref, y0_ref, y1_ref, dn0_ref, dn1_ref, *refs):
    ctx_ref, own_ref, send_ref, grad_ref, ctx_grad_ref, map_grad_ref, gain_grad_ref = refs
    y_refs, dn_refs, ctx_refs = (y0_ref, y1_ref), (dn0_ref, dn1_ref), (ctx_ref,)
    middle = middle_ref[...]
    out = (middle + (y_refs[0][...] + y_refs[1][...])).astype(BF)

    @pl.when(pl.program_id(1) == 0)
    def _():
        own_ref[0] = out

    @pl.when(pl.program_id(1) == 1)
    def _():
        send_ref[0] = out

    dn = dn_refs[0][...] + dn_refs[1][...]
    scale = lax.rsqrt(jnp.mean(middle * middle, axis=1, keepdims=True) + norm_eps)
    unit = middle * scale
    scaled = dn * gain_ref[...]
    inner = jnp.mean(scaled * unit, axis=1, keepdims=True)
    grad = cot_ref[...].astype(F32) + scale * (scaled - unit * inner)
    grad_ref[...] = grad
    low = grad.astype(BF)
    ctx_grad_ref[...] = mm(low, out_w_ref[...], NT).astype(BF)
    map_grad = mm(ctx_refs[0][...], low, TN)
    gain_grad = jnp.sum((dn * unit).reshape(-1, 8, dn.shape[1]), axis=0)
    fresh = pl.program_id(0) + pl.program_id(1) == 0

    @pl.when(fresh)
    def _():
        map_grad_ref[...] = map_grad
        gain_grad_ref[...] = gain_grad

    @pl.when(jnp.logical_not(fresh))
    def _():
        map_grad_ref[...] += map_grad
        gain_grad_ref[...] += gain_grad


def middle_back(core, middle, cot, gain, out_w, y_parts, dn_parts, context, rows):
    tokens, width = middle.shape
    chunk = tokens // rows // 2
    here, row = token_maps(chunk)
    block = pl.BlockSpec((chunk, width), here)
    whole = lambda shape: pl.BlockSpec(shape, lambda r, far, core: (0,) * len(shape))
    half = pl.BlockSpec((1, chunk, width), row)
    return pl.pallas_call(
        middle_kernel,
        grid_spec=pltpu.PrefetchScalarGridSpec(
            num_scalar_prefetch=1,
            grid=(rows, 2),
            in_specs=[block, block, whole((1, width)), whole((width, width))] + [block] * 5,
            out_specs=[half, half, block, block, whole((width, width)), whole((8, width))],
        ),
        out_shape=[
            jax.ShapeDtypeStruct((rows, chunk, width), BF),
            jax.ShapeDtypeStruct((rows, chunk, width), BF),
            jax.ShapeDtypeStruct((tokens, width), F32),
            jax.ShapeDtypeStruct((tokens, width), BF),
            jax.ShapeDtypeStruct((width, width), F32),
            jax.ShapeDtypeStruct((8, width), F32),
        ],
        compiler_params=pltpu.CompilerParams(vmem_limit_bytes=40 << 20),
        cost_estimate=SMALL,
        name="middle_back",
    )(core, *hbm(middle, cot), gain, *hbm(out_w, *y_parts, *dn_parts, context))


def project_kernel(core_ref, normed_ref, own_ref, other_ref, out_ref):
    def each(w_ref):
        for c in range(3):
            out_ref[c] = mm(normed_ref[...], w_ref[c], NN).astype(BF)

    @pl.when(pl.program_id(0) == 0)
    def _():
        each(own_ref)

    @pl.when(pl.program_id(0) == 1)
    def _():
        each(other_ref)


def project(core, normed, own, other):
    tokens, width = normed.shape
    strip = own.shape[2]
    half = pl.BlockSpec((3, width, strip), lambda far, core: (0, 0, 0))
    return pl.pallas_call(
        project_kernel,
        grid_spec=pltpu.PrefetchScalarGridSpec(
            num_scalar_prefetch=1,
            grid=(2,),
            in_specs=[pl.BlockSpec((tokens, width), lambda far, core: (0, 0)), half, half],
            out_specs=pl.BlockSpec(
                (3, tokens, strip), lambda far, core: (0, 0, jnp.bitwise_xor(core[0], far))
            ),
        ),
        out_shape=jax.ShapeDtypeStruct((3, tokens, 2 * strip), BF),
        compiler_params=pltpu.CompilerParams(vmem_limit_bytes=40 << 20),
        cost_estimate=SMALL,
        name="project",
    )(core, normed, own, other)


def entry_kernel(core_ref, hidden_ref, grad_ref, gain_ref, w_own_ref, w_other_ref, *refs):
    grad_refs, (own_ref, send_ref, gain_grad_ref) = refs[:-3], refs[-3:]
    strip = w_own_ref.shape[2]

    def back(low, high):
        total = 0.0
        for c in range(3):
            grads = jnp.concatenate([ref[c] for ref in grad_refs], axis=1)
            total = total + mm(grads[:, :strip], low[c], NT) + mm(grads[:, strip:], high[c], NT)
        hidden = hidden_ref[...].astype(F32)
        scale = lax.rsqrt(jnp.mean(hidden * hidden, axis=1, keepdims=True) + norm_eps)
        unit = hidden * scale
        scaled = total * gain_ref[...]
        inner = jnp.mean(scaled * unit, axis=1, keepdims=True)
        result = grad_ref[...] + scale * (scaled - unit * inner)
        gain_grad = jnp.sum((total * unit).reshape(-1, 8, total.shape[1]), axis=0)
        far = pl.program_id(1)
        fresh = pl.program_id(0) + far == 0

        @pl.when(far == 0)
        def _():
            own_ref[0] = result

        @pl.when(far == 1)
        def _():
            send_ref[0] = result

        @pl.when(fresh)
        def _():
            gain_grad_ref[...] = gain_grad

        @pl.when(jnp.logical_not(fresh))
        def _():
            gain_grad_ref[...] += gain_grad

    @pl.when(core_ref[0] == 0)
    def _():
        back(w_own_ref, w_other_ref)

    @pl.when(core_ref[0] == 1)
    def _():
        back(w_other_ref, w_own_ref)


def entry_back(core, hidden, middle_grad, gain, own, other, grads, rows):
    tokens, width = hidden.shape
    chunk = tokens // rows // 2
    here, row = token_maps(chunk)
    block = pl.BlockSpec((chunk, width), here)
    whole = lambda shape: pl.BlockSpec(shape, lambda r, far, core: (0,) * len(shape))
    half = pl.BlockSpec((1, chunk, width), row)
    part = lambda lanes: pl.BlockSpec((3, chunk, lanes), lambda r, far, core: (0,) + here(r, far, core))
    return pl.pallas_call(
        entry_kernel,
        grid_spec=pltpu.PrefetchScalarGridSpec(
            num_scalar_prefetch=1,
            grid=(rows, 2),
            in_specs=[block, block, whole((1, width))]
            + [whole((3,) + own.shape[1:])] * 2
            + [part(v.shape[2]) for v in grads],
            out_specs=[half, half, whole((8, width))],
        ),
        out_shape=[
            jax.ShapeDtypeStruct((rows, chunk, width), F32),
            jax.ShapeDtypeStruct((rows, chunk, width), F32),
            jax.ShapeDtypeStruct((8, width), F32),
        ],
        compiler_params=pltpu.CompilerParams(vmem_limit_bytes=40 << 20),
        cost_estimate=SMALL,
        name="entry_back",
    )(core, *hbm(hidden, middle_grad), gain, *hbm(own, other, *grads))


def maps_kernel(first_ref, normed_ref, grads_ref, map_ref, *refs):
    keep_ref, send_ref = refs[-2:]
    normed = normed_ref[...]
    one, two, three = (mm(normed, grads_ref[c], TN) for c in range(3))
    four = map_ref[...]

    @pl.when(first_ref[0] == 1)
    def _():
        keep_ref[0], keep_ref[1] = one, two
        send_ref[0], send_ref[1] = three.astype(BF), four.astype(BF)

    @pl.when(first_ref[0] == 0)
    def _():
        keep_ref[0], keep_ref[1] = three, four
        send_ref[0], send_ref[1] = one.astype(BF), two.astype(BF)


def maps_grad(first, normed, grads, map_grad, start, after=()):
    tokens, width = normed.shape
    lanes = grads.shape[2]
    chunk = width // 3
    out = pl.BlockSpec((2, chunk, lanes), lambda s: (0, s, 0))
    return pl.pallas_call(
        maps_kernel,
        grid=(width // chunk,),
        in_specs=[
            pl.BlockSpec(memory_space=pltpu.SMEM),
            pl.BlockSpec((tokens, chunk), lambda s: (0, s)),
            pl.BlockSpec((3, tokens, lanes), lambda s: (0, 0, 0)),
            pl.BlockSpec((chunk, lanes), lambda s: (s, start // lanes)),
        ]
        + [pl.BlockSpec(memory_space=pl.ANY)] * len(after),
        out_specs=[out, out],
        out_shape=[
            jax.ShapeDtypeStruct((2, width, lanes), F32),
            jax.ShapeDtypeStruct((2, width, lanes), BF),
        ],
        compiler_params=pltpu.CompilerParams(vmem_limit_bytes=32 << 20),
        cost_estimate=SMALL,
        name="maps_grad",
    )(first, normed, grads, map_grad, *after)


FOLD = 2


def fold_kernel(order_ref, *refs):
    keep_out, send_out = refs[-2:]
    for j in range(FOLD):
        keep_ref, send_ref, got_keep_ref, got_send_ref = refs[4 * j : 4 * j + 4]
        keep_out[:, j : j + 1] = keep_ref[...] + got_keep_ref[...].astype(F32)
        send_out[:, j : j + 1] = (send_ref[...] + got_send_ref[...].astype(F32)).astype(BF)


def fold(value, got, order):
    many, count, rows, width = value.shape

    def at(which, j):
        return pl.BlockSpec(
            (many, 1, rows, width), lambda s, order: (0, order[which, FOLD * s + j], 0, 0)
        )

    out = pl.BlockSpec((many, FOLD, rows, width), lambda s, order: (0, s, 0, 0))
    shape = (many, count // 2, rows, width)
    return pl.pallas_call(
        fold_kernel,
        grid_spec=pltpu.PrefetchScalarGridSpec(
            num_scalar_prefetch=1,
            grid=(count // 2 // FOLD,),
            in_specs=[at(which, j) for j in range(FOLD) for which in (0, 1, 0, 1)],
            out_specs=[out, out],
        ),
        out_shape=[jax.ShapeDtypeStruct(shape, F32), jax.ShapeDtypeStruct(shape, BF)],
        compiler_params=pltpu.CompilerParams(vmem_limit_bytes=24 << 20),
        cost_estimate=SMALL,
        name="fold",
    )(order, *([value, value, got, got] * FOLD))


class Links:
    def __init__(self, clock):
        self.clock = clock
        self.size = lax.axis_size("dp")
        self.bits = self.size.bit_length() - 1
        self.place = lax.axis_index("dp")
        self.core = lax.axis_index("seq")
        self.first = self.core == 0

    def bit(self, number):
        return lax.rem(lax.div(self.place, 1 << number), 2)

    def turn_bit(self, turn):
        if turn > 1:
            return self.bit(turn)
        return jnp.where(self.first, self.bit(turn), self.bit(1 - turn))

    def swap_seq(self, value):
        return lax.ppermute(value, "seq", [(0, 1), (1, 0)])

    def swap_dp(self, value, turn):
        numbers = (turn, 1 - turn if turn <= 1 else turn)
        pairs = [
            (2 * i + c, 2 * (i ^ (1 << numbers[c])) + c) for i in range(self.size) for c in range(2)
        ]
        return lax.ppermute(value, ("dp", "seq"), pairs)

    def half_places(self):
        quads = np.arange(self.size // 4, dtype=np.int32)[:, None] * 4
        near = np.arange(2, dtype=np.int32)[None, :]
        bit = self.turn_bit(0)

        def places(wanted):
            return jnp.where(
                self.first, quads + near * 2 + wanted, quads + near + wanted * 2
            ).reshape(-1)

        return jnp.stack([places(bit), places(1 - bit)])


    def scatter_first(self, value, got):
        buf, send = fold(value, got, self.clock.after(self.places))
        came = yield send, functools.partial(self.swap_dp, turn=0)
        return buf + came.astype(F32)

    def scatter_rest(self, buf):
        many, _, rows, width = buf.shape
        for turn in range(1, self.bits):
            bit = self.turn_bit(turn)
            view = buf.reshape(many, -1, 2, rows, width)
            cut = lambda b: lax.dynamic_index_in_dim(view, b, 2, keepdims=False)
            send, buf = cut(1 - bit).astype(BF), cut(bit)
            came = yield send, functools.partial(self.swap_dp, turn=turn)
            buf = buf + came.astype(F32)
        return buf

    def scatter(self, value, got):
        buf = yield from self.scatter_first(value, got)
        return (yield from self.scatter_rest(buf))

    def sum_far(self, value):
        for turn in range(2, self.bits):
            low = value.astype(BF)
            came = yield low, functools.partial(self.swap_dp, turn=turn)
            value = low.astype(F32) + came.astype(F32)
        return value

    def order(self, bit, same, other, axis):
        return jnp.where(
            bit == 0, jnp.stack([same, other], axis=axis), jnp.stack([other, same], axis=axis)
        )

    def gather_near(self, buf, at):
        came = yield buf, functools.partial(self.swap_dp, turn=1)
        buf = self.order(self.turn_bit(1), buf, came, at)
        came = yield buf, functools.partial(self.swap_dp, turn=0)
        return jnp.where(
            self.first,
            self.order(self.bit(0), buf, came, at + 1),
            self.order(self.bit(1), buf, came, at),
        )

    def gather(self, value, axis):
        buf, at = value, axis
        for turn in range(self.bits - 1, 1, -1):
            came = yield buf, functools.partial(self.swap_dp, turn=turn)
            buf = self.order(self.bit(turn), buf, came, at)
            at += 1
        buf = yield from self.gather_near(buf, at)
        shape = value.shape
        return buf.reshape(shape[:axis] + (shape[axis] * self.size,) + shape[axis + 1 :])

    def gather_rows(self, buf, last):
        for turn in range(self.bits - 1, 0, -1):
            came = yield buf, functools.partial(self.swap_dp, turn=turn)
            buf = jnp.concatenate([buf, came], axis=1)
        buf = held(buf, last())
        came = yield buf, functools.partial(self.swap_dp, turn=0)
        return buf, came

    def sum_blocks(self, value):
        rows, width = value.shape
        view = value.reshape(2, 2, rows // 4, width)
        cut = lambda b: jnp.where(
            self.first,
            lax.dynamic_index_in_dim(view, b, 1, keepdims=False),
            lax.dynamic_index_in_dim(view, b, 0, keepdims=False),
        )
        bit = self.turn_bit(0)
        came = yield cut(1 - bit).astype(BF), functools.partial(self.swap_dp, turn=0)
        buf = cut(bit) + came.astype(F32)
        bit = self.turn_bit(1)
        half = lambda b: lax.dynamic_index_in_dim(buf, b, 0, keepdims=False)
        came = yield half(1 - bit).astype(BF), functools.partial(self.swap_dp, turn=1)
        buf = yield from self.sum_far(half(bit) + came.astype(F32))
        buf = yield from self.gather_near(buf.astype(BF), 0)
        return buf.reshape(rows, width)

    def all_sum(self, value):
        for turn in range(self.bits):
            came = yield value, functools.partial(self.swap_dp, turn=turn)
            value = value + came
        came = yield value, self.swap_seq
        return value + came

    def by_core(self, own, other, axis):
        return jnp.where(
            self.first,
            jnp.concatenate([own, other], axis=axis),
            jnp.concatenate([other, own], axis=axis),
        )


def held(value, other):
    where = pl.BlockSpec(memory_space=pl.ANY)
    return pl.pallas_call(
        lambda *refs: None,
        in_specs=[where, where],
        out_specs=where,
        out_shape=jax.ShapeDtypeStruct(value.shape, value.dtype),
        input_output_aliases={0: 0},
        cost_estimate=SMALL,
        name="held",
    )(value, other)


def tie(value, others):
    return lax.optimization_barrier((value, *others))[0]


class Order:
    def __init__(self):
        self.last = ()

    def after(self, value):
        return tie(value, self.last) if self.last else value

    def done(self, *values):
        self.last = values


class Chain:
    def __init__(self, order, steps):
        self.clock, self.steps, self.result = order, steps, None
        self.launch(*next(steps))

    def launch(self, send, how, free=False):
        self.flight, self.free = how(send), free
        self.clock.done(send)

    def step(self, count=1):
        for _ in range(count):
            if self.steps is None:
                return
            try:
                came = self.flight if self.free else self.clock.after(self.flight)
                self.launch(*self.steps.send(came))
            except StopIteration as end:
                self.result, self.steps = end.value, None
                self.clock.done(*jax.tree.leaves(self.result))

    def finish(self):
        while self.steps is not None:
            self.step()
        return self.result


def pack_gram(gram):
    count = gram.shape[0] // TILE
    row = lambda i: gram[i * TILE : (i + 1) * TILE, i * TILE :]
    return jnp.concatenate(
        [jnp.concatenate([row(i), row(count - 1 - i)], axis=1) for i in range(count // 2)], axis=0
    )


def unpack_gram(packed):
    count = 2 * packed.shape[0] // TILE
    blocks = {}
    for i in range(count // 2):
        strip = packed[i * TILE : (i + 1) * TILE]
        for j in range(i, count):
            blocks[i, j] = strip[:, (j - i) * TILE : (j - i + 1) * TILE]
        low = count - 1 - i
        for j in range(low, count):
            blocks[low, j] = strip[:, (count - i + j - low) * TILE : (count - i + j - low + 1) * TILE]
    rows = []
    for i in range(count):
        rows.append(
            jnp.concatenate([blocks[i, j] if j >= i else blocks[j, i].T for j in range(count)], axis=1)
        )
    return jnp.concatenate(rows, axis=0)


def muon_kernel(parts, gathered, scaling, *refs):
    sources, (mom_ref, master_ref, out_ref) = refs[:parts], refs[parts:]
    if gathered:
        gram = sum(mm(ref[0], ref[0], TN) for ref in sources)
    else:
        gram = unpack_gram(sources[0][0].astype(F32))
    width = gram.shape[1]
    row = lax.broadcasted_iota(jnp.int32, (width, width), 0)
    column = lax.broadcasted_iota(jnp.int32, (width, width), 1)
    trace = jnp.sum(
        jnp.sum(jnp.where(row == column, gram, 0.0), axis=0, keepdims=True), axis=1, keepdims=True
    )
    scale = 1.0 / (jnp.sqrt(trace) + frob_eps)
    unit = gram * (scale * scale)
    unit_low = unit.astype(BF)
    rest_one = (coeff_b * unit + coeff_c * mm(unit_low, unit_low, NN)).astype(BF)
    cross = mm(rest_one, unit_low, NN)
    second = (
        (coeff_a * coeff_a) * unit
        + (2.0 * coeff_a) * cross
        + mm(rest_one, cross.astype(BF), NN)
    )
    second_low = second.astype(BF)
    rest_two = (coeff_b * second + coeff_c * mm(second_low, second_low, NN)).astype(BF)
    ortho = mom_ref[0] * scale
    ortho = coeff_a * ortho + mm(ortho.astype(BF), rest_one, NN)
    ortho = coeff_a * ortho + mm(ortho.astype(BF), rest_two, NN)
    out_ref[0] = master_ref[0] * (1.0 - muon_rate * muon_decay) - (muon_rate * scaling) * ortho


def gram_kernel(mom_ref, out_ref):
    low = mom_ref[...].astype(BF)
    out_ref[...] = pack_gram(mm(low, low, TN))


def packed_gram(mom):
    width = mom.shape[1]
    return pl.pallas_call(
        gram_kernel,
        out_shape=jax.ShapeDtypeStruct((width // 2, width + TILE), F32),
        compiler_params=pltpu.CompilerParams(vmem_limit_bytes=24 << 20),
        cost_estimate=SMALL,
        name="gram",
    )(mom)


def muon(sources, gathered, mom, master, scaling):
    count, rows, width = mom.shape
    one = lambda shape: pl.BlockSpec((1,) + shape, lambda m: (m, 0, 0))
    return pl.pallas_call(
        functools.partial(muon_kernel, len(sources), gathered, scaling),
        grid=(count,),
        in_specs=[one(v.shape[1:]) for v in sources] + [one((rows, width)), one((rows, width))],
        out_specs=one((rows, width)),
        out_shape=jax.ShapeDtypeStruct(mom.shape, F32),
        compiler_params=pltpu.CompilerParams(vmem_limit_bytes=48 << 20),
        cost_estimate=SMALL,
        name="muon",
    )(*sources, mom, master)


def per_device(
    hidden_in,
    out_grad,
    seg_lengths,
    attn_master,
    ffn_master,
    attn_moment,
    ffn_moment,
    gains,
    gain_first,
    gain_second,
    bias_table,
    bias_first,
    bias_second,
):
    clock = Order()
    links = Links(clock)
    row_len = hidden_in.shape[1] * lax.axis_size("seq")
    heads = bias_table.shape[1]
    core = links.core
    first = links.first
    flag = first.astype(jnp.int32).reshape(1)
    core_at = core.astype(jnp.int32).reshape(1)
    width = attn_master.shape[2]
    pairs = heads // 2
    strip = width // 2
    half = ffn_master.shape[1] // 2
    size = links.size

    def pick(value, count):
        return lax.dynamic_slice_in_dim(value, core * count, count, 0)

    ffn_own = lax.dynamic_slice_in_dim(ffn_master, core * half, half, axis=1).astype(BF)
    ffn_w = lax.all_gather(ffn_own, ("dp", "seq"), axis=1, tiled=True)

    def attn_weights(shard):
        own = yield from links.gather(shard, 1)
        other = yield own, links.swap_seq
        return own, other

    weights = Chain(
        clock,
        attn_weights(
            lax.dynamic_slice_in_dim(attn_master, core * strip, strip, axis=2).astype(BF)
        ),
    )

    def row_halves(value):
        view = value.reshape((2, value.shape[0] // 2) + value.shape[1:])
        own, send = (lax.dynamic_index_in_dim(view, c, 0, keepdims=False) for c in (core, 1 - core))
        return own, send

    hidden_own, hidden_send = row_halves(hidden_in)
    cot_own, cot_send = row_halves(out_grad)
    hidden_other = links.swap_seq(hidden_send)
    cot_other = links.swap_seq(cot_send)
    clock.done(hidden_send, cot_send)
    weights.step()

    rows = hidden_own.shape[0]
    tokens = rows * row_len
    hidden_low = links.by_core(hidden_own, clock.after(hidden_other), 1).reshape(tokens, width)
    hidden = hidden_low.astype(F32)
    scale_one = lax.rsqrt(jnp.mean(hidden * hidden, axis=-1, keepdims=True) + norm_eps)
    normed = (hidden * scale_one * gains[0]).astype(BF)
    clock.done(normed)
    weights.step()

    seg_rows = lax.dynamic_slice_in_dim(seg_lengths, core * rows, rows, 0)
    seg_ends = jnp.cumsum(seg_rows, axis=-1)
    places = jnp.arange(row_len, dtype=jnp.int32)
    seg_full = jnp.sum((places[None, :, None] >= seg_ends[:, None, :]).astype(jnp.int32), axis=-1)
    valid = (seg_full < seg_rows.shape[1]).reshape(tokens, 1)
    seg_col = seg_full.reshape(rows, row_len, 1)
    seg_row = seg_full.reshape(rows, 1, row_len)
    cot_rows = links.by_core(cot_own, clock.after(cot_other), 1).reshape(tokens, width)
    cotangent = jnp.where(valid, cot_rows, jnp.zeros((), BF))
    onehot = offset_onehot(bias_table.shape[0])
    onehot_rev = np.concatenate([onehot[-2::-1], onehot[-1:]], axis=0)
    trev = exact_dot(onehot_rev, bias_table, "mb,bh->hm").reshape(heads // 2, 2, 4 * TILE)
    links.places = links.half_places()
    clock.done(cotangent, seg_col, seg_row, trev, links.places)
    weights.step()

    moment_attn = pick(attn_moment, 2)
    w_own, w_other = weights.finish()
    proj = project(core_at, normed, w_own, w_other)
    out_w = links.by_core(w_own[3], w_other[3], 1)
    context, lse = attend(proj, trev, seg_col, seg_row, rows, row_len, 0)

    middle = hidden + mm(context, out_w, NN)
    scale_two = lax.rsqrt(jnp.mean(middle * middle, axis=-1, keepdims=True) + norm_eps)
    normed_two = (middle * scale_two * gains[1]).astype(BF)

    def ffn_first(keep, send):
        view = (1, size, half, width)
        came = yield send, links.swap_seq, True
        return (yield from links.scatter_first(keep.reshape(view), came.reshape(view)))

    def ffn_rest(first_part, second_part):
        buf = jnp.concatenate([first_part, second_part], axis=2)
        total = yield from links.scatter_rest(buf)
        return total.reshape(1, 2 * half, width)

    y_parts, dn_parts, sums = [], [], []
    clock.done(normed_two)
    for p in range(2):
        y, dn, keep, send = ffn(clock.after(flag), normed_two, cotangent, ffn_w, size, p)
        y_parts.append(y)
        dn_parts.append(dn)
        sums.append(Chain(clock, ffn_first(keep, send)))
    one, two = sums
    one.step()
    out_own, out_send, middle_grad, context_grad, out_map_grad, gain_two_part = middle_back(
        clock.after(core_at), middle, cotangent, gains[1:2], out_w, y_parts, dn_parts, context, rows
    )
    clock.done(gain_two_part)

    done_grads, diag = [], []
    near = [0, 0]
    sizes = (pairs - pairs // 3, pairs // 3)

    def back(group, grads, count=2):
        start, member = sum(sizes[:group]), near[group]
        near[group] += count
        grads, diag_m = attend_back(
            proj,
            trev,
            seg_col,
            clock.after(seg_row),
            lse,
            context_grad,
            rows,
            row_len,
            start + member,
            member,
            count,
            sizes[group],
            grads,
        )
        diag.append(diag_m)
        clock.done(diag_m)
        return grads

    def maps(group, grads):
        done_grads.append(grads)
        keep, send = maps_grad(
            clock.after(flag), normed, grads, out_map_grad, sum(sizes[:group]) * TILE
        )
        clock.done(send)
        return keep, send

    def attn_first(group, keep, send):
        view = (2, size, width // size, sizes[group] * TILE)
        came = yield send, links.swap_seq, True
        return (yield from links.scatter_first(keep.reshape(view), came.reshape(view)))

    def attn_rest(first_group, second_group):
        buf = jnp.concatenate([first_group, second_group], axis=3)
        total = yield from links.scatter_rest(buf)
        grad = total.reshape(2, width // size, width)
        mom = muon_beta * moment_attn + grad
        whole = yield from links.gather_rows(mom.astype(BF), lambda: gram.result)
        return grad, mom, whole

    two.step()
    grads = back(0, None)
    grads = back(0, grads)
    first_part, second_part = one.finish(), two.finish()
    units = Chain(clock, ffn_rest(first_part, second_part))
    three = Chain(clock, attn_first(0, *maps(0, grads)))
    grads = back(1, None)
    three.step()
    four = Chain(clock, attn_first(1, *maps(1, grads)))
    units.step()
    four.step()
    grad_own, grad_send, gain_one_part = entry_back(
        clock.after(core_at), hidden_low, middle_grad, gains[0:1], w_own, w_other, done_grads, rows
    )
    clock.done(gain_one_part)
    first_group, second_group = three.finish(), four.finish()
    maps_sum = Chain(clock, attn_rest(first_group, second_group))
    units.step()
    out_other = links.swap_seq(clock.after(out_send))
    diag = jnp.concatenate(diag, axis=0).reshape(heads, 4 * TILE)
    table_grad = exact_dot(onehot_rev, diag, "mb,hm->bh")
    small = jnp.concatenate(
        [
            jnp.sum(gain_one_part, axis=0),
            jnp.sum(gain_two_part, axis=0),
            table_grad.reshape(-1),
        ]
    )
    small = Chain(clock, links.all_sum(small))
    maps_sum.step()
    hidden_out = links.by_core(out_own, clock.after(out_other), 0)
    clock.done(hidden_out)
    maps_sum.step()
    ffn_grad = units.finish()
    mom_ffn = muon_beta * pick(ffn_moment, 1) + ffn_grad
    gram = Chain(clock, links.sum_blocks(packed_gram(mom_ffn[0])))
    small.step()
    grad_other = links.swap_seq(clock.after(grad_send))
    maps_sum.step()
    gram.step()
    small.step()
    gram.step()
    grad_tokens = links.by_core(grad_own, clock.after(grad_other), 0)
    clock.done(grad_tokens)
    maps_sum.step()
    small.step()
    gram.step()
    ffn_other = links.swap_seq(clock.after(ffn_grad))
    maps_sum.step()
    gram.step()
    ffn_mom = muon_beta * ffn_moment + links.by_core(ffn_grad, clock.after(ffn_other), 0)
    clock.done(ffn_mom)
    gram.step()
    small.step()
    gram.finish()
    maps_sum.step()
    if links.bits > 4:
        maps_sum.step(2 * links.bits - 8)
    gram_ffn, small = gram.finish(), small.finish()
    gain_sum = small[: 2 * width].reshape(2, width)
    table_sum = small[2 * width :].reshape(table_grad.shape)
    new_ffn = muon(
        [gram_ffn[None]],
        False,
        clock.after(mom_ffn),
        pick(ffn_master, 1),
        math.sqrt(max(1.0, FF / D)),
    )
    clock.done(new_ffn)
    attn_grad, mom_attn, attn_whole = maps_sum.finish()
    attn_other = links.swap_seq(attn_grad)
    new_attn = muon(attn_whole, True, mom_attn, pick(attn_master, 2), 1.0)
    attn_mom = muon_beta * attn_moment + links.by_core(attn_grad, attn_other, 0)
    new_gains, new_gain_first, new_gain_second = adamw(gains, gain_first, gain_second, gain_sum)
    new_bias, new_bias_first, new_bias_second = adamw(
        bias_table, bias_first, bias_second, table_sum
    )
    return (
        hidden_out,
        grad_tokens,
        new_attn,
        attn_mom,
        new_ffn,
        ffn_mom,
        new_gains,
        new_gain_first,
        new_gain_second,
        new_bias,
        new_bias_first,
        new_bias_second,
    )


def solution(mesh):
    in_specs = (
        P("dp", "seq", None),
        P("dp", "seq", None),
        P("dp", None),
        P(None, "dp", None),
        P(None, "dp", None),
        P(None, "dp", None),
        P(None, "dp", None),
        P(),
        P(),
        P(),
        P(),
        P(),
        P(),
    )
    out_specs = (
        P("dp", "seq", None),
        P("dp", "seq", None),
        P("seq", "dp", None),
        P(None, "dp", None),
        P("seq", "dp", None),
        P(None, "dp", None),
        P(),
        P(),
        P(),
        P(),
        P(),
        P(),
    )
    return jax.shard_map(
        per_device, mesh=mesh, in_specs=in_specs, out_specs=out_specs, check_vma=False
    )
```

```python
import functools
import math

import jax
import jax.numpy as jnp
import numpy as np
from jax import lax
from jax.experimental import pallas as pl
from jax.experimental.pallas import tpu as pltpu
from jax.sharding import PartitionSpec as P

D = 768
FF = 3072
NS_STEPS = 2
STEP = 10
TILE = 128

bucket_edges = (1, 2, 3, 4, 5, 6, 7, 8, 12, 16, 23, 32, 46, 64, 91)
norm_eps = 1e-06
masked_score = -1000000000.0
coeff_a = 3.4445
coeff_b = -4.775
coeff_c = 2.0315
frob_eps = 1e-07
muon_beta = 0.95
muon_rate = 0.6
muon_decay = 0.01
adam_one = 0.9
adam_two = 0.999
adam_rate = 0.3
adam_eps = 1e-08

BF = jnp.bfloat16
F32 = jnp.float32
NT = (((1,), (1,)), ((), ()))
NN = (((1,), (0,)), ((), ()))
TN = (((0,), (0,)), ((), ()))
SMALL = pl.CostEstimate(flops=1000, bytes_accessed=1000, transcendentals=0)


def mm(left, right, dims):
    return lax.dot_general(left, right, dims, preferred_element_type=F32)


def hbm(*values):
    return tuple(pltpu.with_memory_space_constraint(v, pltpu.HBM) for v in values)


def exact_dot(left, right, form):
    return jnp.einsum(form, left, right, precision=lax.Precision.HIGHEST)


def offset_onehot(buckets):
    offset = np.arange(4 * TILE) - (2 * TILE - 1)
    bucket = np.where(offset > 0, 16, 0)
    for edge_value in bucket_edges:
        bucket = bucket + (np.abs(offset) >= edge_value)
    hot = (bucket[:, None] == np.arange(buckets)).astype(np.float32)
    hot[-1] = 0.0
    return hot


def norm_back(scaled_grad, unit, scale):
    return scale * (scaled_grad - unit * jnp.mean(scaled_grad * unit, axis=-1, keepdims=True))


def adamw(param, first_in, second_in, grad):
    first_new = adam_one * first_in + (1.0 - adam_one) * grad
    second_new = adam_two * second_in + (1.0 - adam_two) * grad * grad
    fix_one = 1.0 - adam_one**STEP
    fix_two = 1.0 - adam_two**STEP
    update = first_new / fix_one / (jnp.sqrt(second_new / fix_two) + adam_eps)
    return (param - adam_rate * update, first_new, second_new)


def skew_tile(vector):
    width = vector.shape[1]
    base = pltpu.roll(jnp.broadcast_to(vector, (8, width)), width - (TILE - 1), axis=1)
    row = lax.broadcasted_iota(jnp.int32, (8, width), 0)
    head = base
    for i in range(1, 8):
        head = jnp.where(row == i, pltpu.roll(base, i, axis=1), head)
    pieces = [head] + [pltpu.roll(head, 8 * g, axis=1) for g in range(1, TILE // 8)]
    return jnp.concatenate(pieces, axis=0)


def unskew_sum(tile):
    width = tile.shape[1]
    rows = tile.shape[0]
    while rows > 8:
        half = rows // 2
        tile = tile[:half] + pltpu.roll(tile[half:], width - half, axis=1)
        rows = half
    row = lax.broadcasted_iota(jnp.int32, (8, width), 0)
    total = jnp.where(row == 0, tile, 0.0)
    for i in range(1, 8):
        total = total + jnp.where(row == i, pltpu.roll(tile, width - i, axis=1), 0.0)
    return pltpu.roll(jnp.broadcast_to(jnp.sum(total, axis=0, keepdims=True), (8, width)), TILE - 1, axis=1)[
        0:1
    ]


def bias_column(bias_ref, far, a, first_block, count, blocks):
    columns = []
    for qb in range(first_block, first_block + count):
        pieces = []
        for kb in range(blocks):
            diff = qb - kb
            if diff <= -2:
                pieces.append(far[a][0])
            elif diff >= 2:
                pieces.append(far[a][1])
            else:
                pieces.append(bias_ref[a, :, (diff + 1) * TILE : (diff + 2) * TILE])
        columns.append(jnp.concatenate(pieces, axis=0))
    return jnp.concatenate(columns, axis=1)


def bias_setup(trev_ref, bias_ref):
    far = []
    for a in range(2):
        vector = trev_ref[0, a : a + 1, :]
        bias_ref[a] = skew_tile(vector)
        far.append(
            (
                jnp.broadcast_to(vector[:, 0:1], (TILE, TILE)),
                jnp.broadcast_to(vector[:, 4 * TILE - 2 : 4 * TILE - 1], (TILE, TILE)),
            )
        )
    return far


def attend_kernel(
    rows, length, wide, extra, trev_ref, segk_ref, segq_ref, q_ref, k_ref, v_ref, *refs
):
    ctx_ref, lse_ref, bias_ref = refs[extra:]
    blocks = length // TILE
    lane = lax.broadcasted_iota(jnp.int32, (wide, TILE), 1)
    low_half = lane < TILE // 2
    far = bias_setup(trev_ref, bias_ref)
    for r in range(rows):
        span = slice(r * length, (r + 1) * length)
        keys = k_ref[0, span, :]
        values = v_ref[0, span, :]
        seg_k = segk_ref[r]
        for qt in range(length // wide):
            at = slice(r * length + qt * wide, r * length + (qt + 1) * wide)
            query = q_ref[0, at, :]
            same = seg_k == segq_ref[r, :, qt * wide : (qt + 1) * wide]
            outs = []
            for a in range(2):
                mine = low_half if a == 0 else jnp.logical_not(low_half)
                raw = mm(keys, jnp.where(mine, query, jnp.zeros_like(query)), NT)
                step = wide // TILE
                raw = raw + bias_column(bias_ref, far, a, qt * step, step, blocks)
                scores = jnp.where(same, raw, masked_score)
                row_max = jnp.max(scores, axis=0, keepdims=True)
                exp_scores = jnp.exp(scores - row_max)
                total = jnp.sum(exp_scores, axis=0, keepdims=True)
                probs = (exp_scores * (1.0 / total)).astype(BF)
                outs.append(mm(probs, values, TN))
                lse_ref[0, a : a + 1, at] = row_max + jnp.log(total)
            ctx_ref[at, :] = jnp.where(low_half, outs[0], outs[1]).astype(BF)


def attend(proj, trev, seg_col, seg_row, rows, length, first_pair, after=()):
    tokens = proj.shape[1]
    pairs = proj.shape[2] // TILE
    whole = lambda shape: pl.BlockSpec(shape, lambda p: (0,) * len(shape))
    part = lambda c: pl.BlockSpec((1, tokens, TILE), lambda p: (c, 0, p))
    return pl.pallas_call(
        functools.partial(attend_kernel, rows, length, 2 * TILE, len(after)),
        grid=(pairs,),
        in_specs=[
            pl.BlockSpec((1, 2, 4 * TILE), lambda p: (p + first_pair, 0, 0)),
            whole((rows, length, 1)),
            whole((rows, 1, length)),
            part(0),
            part(1),
            part(2),
        ]
        + [pl.BlockSpec(memory_space=pl.ANY)] * len(after),
        out_specs=[
            pl.BlockSpec((tokens, TILE), lambda p: (0, p)),
            pl.BlockSpec((1, 2, tokens), lambda p: (p, 0, 0)),
        ],
        out_shape=[
            jax.ShapeDtypeStruct((tokens, pairs * TILE), BF),
            jax.ShapeDtypeStruct((pairs, 2, tokens), F32),
        ],
        scratch_shapes=[pltpu.VMEM((2, TILE, 4 * TILE), F32)],
        compiler_params=pltpu.CompilerParams(vmem_limit_bytes=40 << 20),
        cost_estimate=SMALL,
        name="attend",
    )(trev, seg_col, seg_row, proj, proj, proj, *after)


def attend_back_kernel(
    rows,
    length,
    wide,
    extra,
    trev_ref,
    segk_ref,
    segq_ref,
    lse_ref,
    q_ref,
    k_ref,
    v_ref,
    do_ref,
    *refs,
):
    grad_ref, diag_ref, bias_ref, acc_ref = refs[extra:]
    blocks = length // TILE
    lane = lax.broadcasted_iota(jnp.int32, (wide, TILE), 1)
    low_half = lane < TILE // 2
    lane_row = lax.broadcasted_iota(jnp.int32, (1, 4 * TILE), 1)
    far = bias_setup(trev_ref, bias_ref)
    sums = [[jnp.zeros((8, TILE), F32) for _ in range(2)] for _ in range(2)]
    acc_ref[...] = jnp.zeros_like(acc_ref)
    step = wide // TILE
    for r in range(rows):
        span = slice(r * length, (r + 1) * length)
        keys = k_ref[0, span, :]
        values = v_ref[0, span, :]
        seg_k = segk_ref[r]
        key_grad = jnp.zeros((length, TILE), F32)
        value_grad = jnp.zeros((length, TILE), F32)
        for qt in range(length // wide):
            at = slice(r * length + qt * wide, r * length + (qt + 1) * wide)
            query = q_ref[0, at, :]
            do = do_ref[at, :]
            same = seg_k == segq_ref[r, :, qt * wide : (qt + 1) * wide]
            query_grads = []
            for a in range(2):
                mine = low_half if a == 0 else jnp.logical_not(low_half)
                query_a = jnp.where(mine, query, jnp.zeros_like(query))
                do_a = jnp.where(mine, do, jnp.zeros_like(do))
                raw = mm(keys, query_a, NT)
                raw = raw + bias_column(bias_ref, far, a, qt * step, step, blocks)
                scores = jnp.where(same, raw, masked_score)
                probs = jnp.exp(scores - lse_ref[0, a : a + 1, at])
                probs_grad = mm(values, do_a, NT)
                weighted = probs * probs_grad
                inner = jnp.sum(weighted, axis=0, keepdims=True)
                score_grad = (weighted - probs * inner).astype(BF)
                value_grad = value_grad + mm(probs.astype(BF), do_a, NN)
                key_grad = key_grad + mm(score_grad, query_a, NN)
                query_grads.append(mm(score_grad, keys, TN))
                for qs in range(step):
                    for kb in range(blocks):
                        diff = qt * step + qs - kb
                        piece = score_grad[
                            kb * TILE : (kb + 1) * TILE, qs * TILE : (qs + 1) * TILE
                        ].astype(F32)
                        if abs(diff) >= 2:
                            side = 0 if diff < 0 else 1
                            sums[a][side] = sums[a][side] + jnp.sum(
                                piece.reshape(TILE // 8, 8, TILE), axis=0
                            )
                        else:
                            acc_ref[a, :, (diff + 1) * TILE : (diff + 2) * TILE] += piece
            grad_ref[0, at, :] = jnp.where(low_half, query_grads[0], query_grads[1]).astype(BF)
        grad_ref[1, span, :] = key_grad.astype(BF)
        grad_ref[2, span, :] = value_grad.astype(BF)
    for a in range(2):
        near = unskew_sum(acc_ref[a])
        ends = [
            jnp.sum(jnp.sum(sums[a][side], axis=1, keepdims=True), axis=0, keepdims=True)
            for side in range(2)
        ]
        diag_ref[0, a : a + 1, :] = (
            near
            + jnp.where(lane_row == 0, ends[0], 0.0)
            + jnp.where(lane_row == 4 * TILE - 2, ends[1], 0.0)
        )


def attend_back(
    proj, trev, seg_col, seg_row, lse_rows, do, rows, length, pair, member, count, pairs, carried
):
    tokens = proj.shape[1]
    lanes = pairs * TILE
    whole = lambda shape: pl.BlockSpec(shape, lambda p: (0,) * len(shape))
    part = lambda c: pl.BlockSpec((1, tokens, TILE), lambda p: (c, 0, pair + p))
    one = lambda size, which: pl.BlockSpec((1, 2, size), lambda p: (which + p, 0, 0))
    extras = () if carried is None else (carried,)
    return pl.pallas_call(
        functools.partial(attend_back_kernel, rows, length, 2 * TILE, len(extras)),
        grid=(count,),
        in_specs=[
            one(4 * TILE, pair),
            whole((rows, length, 1)),
            whole((rows, 1, length)),
            one(tokens, pair),
            part(0),
            part(1),
            part(2),
            pl.BlockSpec((tokens, TILE), lambda p: (0, pair + p)),
        ]
        + [pl.BlockSpec(memory_space=pl.ANY)] * len(extras),
        out_specs=[
            pl.BlockSpec((3, tokens, TILE), lambda p: (0, 0, member + p)),
            one(4 * TILE, 0),
        ],
        out_shape=[
            jax.ShapeDtypeStruct((3, tokens, lanes), BF),
            jax.ShapeDtypeStruct((count, 2, 4 * TILE), F32),
        ],
        scratch_shapes=[
            pltpu.VMEM((2, TILE, 4 * TILE), F32),
            pltpu.VMEM((2, TILE, 4 * TILE), F32),
        ],
        input_output_aliases={} if carried is None else {8: 0},
        compiler_params=pltpu.CompilerParams(vmem_limit_bytes=48 << 20),
        cost_estimate=SMALL,
        name="attend_back",
    )(trev, seg_col, seg_row, lse_rows, *hbm(proj, proj, proj, do), *extras)


def ffn_kernel(extra, first_ref, normed_ref, cot_ref, w_ref, *refs):
    y_ref, dn_ref, keep_ref, send_ref = refs[extra:]
    step = pl.program_id(0)
    width = normed_ref.shape[1]

    @pl.when(step == 0)
    def _():
        y_ref[...] = jnp.zeros_like(y_ref)
        dn_ref[...] = jnp.zeros_like(dn_ref)

    w_in = w_ref[0].reshape(-1, width)
    w_out = w_ref[1].reshape(-1, width)
    normed = normed_ref[...]
    cot = cot_ref[...]
    pre = mm(w_in, normed, NT)
    act_grad = mm(w_out, cot, NT)
    square = pre * pre
    root = math.sqrt(2.0 / math.pi)
    tanh = jnp.tanh(pre * (root + (root * 0.044715) * square))
    half = 0.5 * (1.0 + tanh)
    act = (pre * half).astype(BF)
    slope = half + (0.5 * pre) * (1.0 - tanh * tanh) * (root + (3.0 * root * 0.044715) * square)
    pre_low = (act_grad * slope).astype(BF)
    y_ref[...] += mm(act, w_out, TN)
    dn_ref[...] += mm(pre_low, w_in, TN)
    down = mm(act, cot, NN)
    up = mm(pre_low, normed, NN)

    @pl.when(first_ref[0] == 1)
    def _():
        keep_ref[...] = up
        send_ref[...] = down.astype(BF)

    @pl.when(first_ref[0] == 0)
    def _():
        keep_ref[...] = down
        send_ref[...] = up.astype(BF)


def ffn(first, normed, cot, weights, places, part, after=()):
    tokens, width = normed.shape
    units = weights.shape[1] // 2
    half = units // places
    view = weights.reshape(2, places, 2, half, width)
    if half % 16 == 0:
        blocks = 384 // half
        chunk = blocks * half
        w_spec = pl.BlockSpec((2, blocks, None, half, width), lambda s: (0, s, part, 0, 0))
    else:
        chunk = 512
        view = view[:, :, part].reshape(2, units, width)
        w_spec = pl.BlockSpec((2, chunk, width), lambda s: (0, s, 0))
    whole = lambda shape, mode=None: pl.BlockSpec(
        shape, lambda s: (0,) * len(shape), pipeline_mode=mode
    )
    block = pl.BlockSpec((chunk, width), lambda s: (s, 0))
    once = pl.Buffered(1)
    return pl.pallas_call(
        functools.partial(ffn_kernel, len(after)),
        grid=(units // chunk,),
        in_specs=[
            pl.BlockSpec(memory_space=pltpu.SMEM),
            whole((tokens, width), once),
            whole((tokens, width), once),
            w_spec,
        ]
        + [pl.BlockSpec(memory_space=pl.ANY)] * len(after),
        out_specs=[whole((tokens, width)), whole((tokens, width)), block, block],
        out_shape=[
            jax.ShapeDtypeStruct((tokens, width), F32),
            jax.ShapeDtypeStruct((tokens, width), F32),
            jax.ShapeDtypeStruct((units, width), F32),
            jax.ShapeDtypeStruct((units, width), BF),
        ],
        compiler_params=pltpu.CompilerParams(vmem_limit_bytes=52 << 20),
        cost_estimate=SMALL,
        name="ffn",
    )(first, normed, cot, view, *after)


def token_maps(length):
    block = lambda r, far, core: 2 * r + jnp.bitwise_xor(core[0], far)
    return lambda r, far, core: (block(r, far, core), 0), lambda r, far, core: (r, 0, 0)


def middle_kernel(core_ref, middle_ref, cot_ref, gain_ref, out_w_ref, y0_ref, y1_ref, dn0_ref, dn1_ref, *refs):
    ctx_ref, own_ref, send_ref, grad_ref, ctx_grad_ref, map_grad_ref, gain_grad_ref = refs
    y_refs, dn_refs, ctx_refs = (y0_ref, y1_ref), (dn0_ref, dn1_ref), (ctx_ref,)
    middle = middle_ref[...]
    out = (middle + (y_refs[0][...] + y_refs[1][...])).astype(BF)

    @pl.when(pl.program_id(1) == 0)
    def _():
        own_ref[0] = out

    @pl.when(pl.program_id(1) == 1)
    def _():
        send_ref[0] = out

    dn = dn_refs[0][...] + dn_refs[1][...]
    scale = lax.rsqrt(jnp.mean(middle * middle, axis=1, keepdims=True) + norm_eps)
    unit = middle * scale
    scaled = dn * gain_ref[...]
    inner = jnp.mean(scaled * unit, axis=1, keepdims=True)
    grad = cot_ref[...].astype(F32) + scale * (scaled - unit * inner)
    grad_ref[...] = grad
    low = grad.astype(BF)
    ctx_grad_ref[...] = mm(low, out_w_ref[...], NT).astype(BF)
    map_grad = mm(ctx_refs[0][...], low, TN)
    gain_grad = jnp.sum((dn * unit).reshape(-1, 8, dn.shape[1]), axis=0)
    fresh = pl.program_id(0) + pl.program_id(1) == 0

    @pl.when(fresh)
    def _():
        map_grad_ref[...] = map_grad
        gain_grad_ref[...] = gain_grad

    @pl.when(jnp.logical_not(fresh))
    def _():
        map_grad_ref[...] += map_grad
        gain_grad_ref[...] += gain_grad


def middle_back(core, middle, cot, gain, out_w, y_parts, dn_parts, context, rows):
    tokens, width = middle.shape
    chunk = tokens // rows // 2
    here, row = token_maps(chunk)
    block = pl.BlockSpec((chunk, width), here)
    whole = lambda shape: pl.BlockSpec(shape, lambda r, far, core: (0,) * len(shape))
    half = pl.BlockSpec((1, chunk, width), row)
    return pl.pallas_call(
        middle_kernel,
        grid_spec=pltpu.PrefetchScalarGridSpec(
            num_scalar_prefetch=1,
            grid=(rows, 2),
            in_specs=[block, block, whole((1, width)), whole((width, width))] + [block] * 5,
            out_specs=[half, half, block, block, whole((width, width)), whole((8, width))],
        ),
        out_shape=[
            jax.ShapeDtypeStruct((rows, chunk, width), BF),
            jax.ShapeDtypeStruct((rows, chunk, width), BF),
            jax.ShapeDtypeStruct((tokens, width), F32),
            jax.ShapeDtypeStruct((tokens, width), BF),
            jax.ShapeDtypeStruct((width, width), F32),
            jax.ShapeDtypeStruct((8, width), F32),
        ],
        compiler_params=pltpu.CompilerParams(vmem_limit_bytes=40 << 20),
        cost_estimate=SMALL,
        name="middle_back",
    )(core, *hbm(middle, cot), gain, *hbm(out_w, *y_parts, *dn_parts, context))


def project_kernel(core_ref, normed_ref, own_ref, other_ref, out_ref):
    def each(w_ref):
        for c in range(3):
            out_ref[c] = mm(normed_ref[...], w_ref[c], NN).astype(BF)

    @pl.when(pl.program_id(0) == 0)
    def _():
        each(own_ref)

    @pl.when(pl.program_id(0) == 1)
    def _():
        each(other_ref)


def project(core, normed, own, other):
    tokens, width = normed.shape
    strip = own.shape[2]
    half = pl.BlockSpec((3, width, strip), lambda far, core: (0, 0, 0))
    return pl.pallas_call(
        project_kernel,
        grid_spec=pltpu.PrefetchScalarGridSpec(
            num_scalar_prefetch=1,
            grid=(2,),
            in_specs=[pl.BlockSpec((tokens, width), lambda far, core: (0, 0)), half, half],
            out_specs=pl.BlockSpec(
                (3, tokens, strip), lambda far, core: (0, 0, jnp.bitwise_xor(core[0], far))
            ),
        ),
        out_shape=jax.ShapeDtypeStruct((3, tokens, 2 * strip), BF),
        compiler_params=pltpu.CompilerParams(vmem_limit_bytes=40 << 20),
        cost_estimate=SMALL,
        name="project",
    )(core, normed, own, other)


def entry_kernel(core_ref, hidden_ref, grad_ref, gain_ref, w_own_ref, w_other_ref, *refs):
    grad_refs, (own_ref, send_ref, gain_grad_ref) = refs[:-3], refs[-3:]
    strip = w_own_ref.shape[2]

    def back(low, high):
        total = 0.0
        for c in range(3):
            grads = jnp.concatenate([ref[c] for ref in grad_refs], axis=1)
            total = total + mm(grads[:, :strip], low[c], NT) + mm(grads[:, strip:], high[c], NT)
        hidden = hidden_ref[...].astype(F32)
        scale = lax.rsqrt(jnp.mean(hidden * hidden, axis=1, keepdims=True) + norm_eps)
        unit = hidden * scale
        scaled = total * gain_ref[...]
        inner = jnp.mean(scaled * unit, axis=1, keepdims=True)
        result = grad_ref[...] + scale * (scaled - unit * inner)
        gain_grad = jnp.sum((total * unit).reshape(-1, 8, total.shape[1]), axis=0)
        far = pl.program_id(1)
        fresh = pl.program_id(0) + far == 0

        @pl.when(far == 0)
        def _():
            own_ref[0] = result

        @pl.when(far == 1)
        def _():
            send_ref[0] = result

        @pl.when(fresh)
        def _():
            gain_grad_ref[...] = gain_grad

        @pl.when(jnp.logical_not(fresh))
        def _():
            gain_grad_ref[...] += gain_grad

    @pl.when(core_ref[0] == 0)
    def _():
        back(w_own_ref, w_other_ref)

    @pl.when(core_ref[0] == 1)
    def _():
        back(w_other_ref, w_own_ref)


def entry_back(core, hidden, middle_grad, gain, own, other, grads, rows):
    tokens, width = hidden.shape
    chunk = tokens // rows // 2
    here, row = token_maps(chunk)
    block = pl.BlockSpec((chunk, width), here)
    whole = lambda shape: pl.BlockSpec(shape, lambda r, far, core: (0,) * len(shape))
    half = pl.BlockSpec((1, chunk, width), row)
    part = lambda lanes: pl.BlockSpec((3, chunk, lanes), lambda r, far, core: (0,) + here(r, far, core))
    return pl.pallas_call(
        entry_kernel,
        grid_spec=pltpu.PrefetchScalarGridSpec(
            num_scalar_prefetch=1,
            grid=(rows, 2),
            in_specs=[block, block, whole((1, width))]
            + [whole((3,) + own.shape[1:])] * 2
            + [part(v.shape[2]) for v in grads],
            out_specs=[half, half, whole((8, width))],
        ),
        out_shape=[
            jax.ShapeDtypeStruct((rows, chunk, width), F32),
            jax.ShapeDtypeStruct((rows, chunk, width), F32),
            jax.ShapeDtypeStruct((8, width), F32),
        ],
        compiler_params=pltpu.CompilerParams(vmem_limit_bytes=40 << 20),
        cost_estimate=SMALL,
        name="entry_back",
    )(core, *hbm(hidden, middle_grad), gain, *hbm(own, other, *grads))


def maps_kernel(first_ref, normed_ref, grads_ref, map_ref, *refs):
    keep_ref, send_ref = refs[-2:]
    normed = normed_ref[...]
    one, two, three = (mm(normed, grads_ref[c], TN) for c in range(3))
    four = map_ref[...]

    @pl.when(first_ref[0] == 1)
    def _():
        keep_ref[0], keep_ref[1] = one, two
        send_ref[0], send_ref[1] = three.astype(BF), four.astype(BF)

    @pl.when(first_ref[0] == 0)
    def _():
        keep_ref[0], keep_ref[1] = three, four
        send_ref[0], send_ref[1] = one.astype(BF), two.astype(BF)


def maps_grad(first, normed, grads, map_grad, start, after=()):
    tokens, width = normed.shape
    lanes = grads.shape[2]
    chunk = width // 3
    out = pl.BlockSpec((2, chunk, lanes), lambda s: (0, s, 0))
    return pl.pallas_call(
        maps_kernel,
        grid=(width // chunk,),
        in_specs=[
            pl.BlockSpec(memory_space=pltpu.SMEM),
            pl.BlockSpec((tokens, chunk), lambda s: (0, s)),
            pl.BlockSpec((3, tokens, lanes), lambda s: (0, 0, 0)),
            pl.BlockSpec((chunk, lanes), lambda s: (s, start // lanes)),
        ]
        + [pl.BlockSpec(memory_space=pl.ANY)] * len(after),
        out_specs=[out, out],
        out_shape=[
            jax.ShapeDtypeStruct((2, width, lanes), F32),
            jax.ShapeDtypeStruct((2, width, lanes), BF),
        ],
        compiler_params=pltpu.CompilerParams(vmem_limit_bytes=32 << 20),
        cost_estimate=SMALL,
        name="maps_grad",
    )(first, normed, grads, map_grad, *after)


FOLD = 2


def fold_kernel(order_ref, *refs):
    keep_out, send_out = refs[-2:]
    for j in range(FOLD):
        keep_ref, send_ref, got_keep_ref, got_send_ref = refs[4 * j : 4 * j + 4]
        keep_out[:, j : j + 1] = keep_ref[...] + got_keep_ref[...].astype(F32)
        send_out[:, j : j + 1] = (send_ref[...] + got_send_ref[...].astype(F32)).astype(BF)


def fold(value, got, order):
    many, count, rows, width = value.shape

    def at(which, j):
        return pl.BlockSpec(
            (many, 1, rows, width), lambda s, order: (0, order[which, FOLD * s + j], 0, 0)
        )

    out = pl.BlockSpec((many, FOLD, rows, width), lambda s, order: (0, s, 0, 0))
    shape = (many, count // 2, rows, width)
    return pl.pallas_call(
        fold_kernel,
        grid_spec=pltpu.PrefetchScalarGridSpec(
            num_scalar_prefetch=1,
            grid=(count // 2 // FOLD,),
            in_specs=[at(which, j) for j in range(FOLD) for which in (0, 1, 0, 1)],
            out_specs=[out, out],
        ),
        out_shape=[jax.ShapeDtypeStruct(shape, F32), jax.ShapeDtypeStruct(shape, BF)],
        compiler_params=pltpu.CompilerParams(vmem_limit_bytes=24 << 20),
        cost_estimate=SMALL,
        name="fold",
    )(order, *([value, value, got, got] * FOLD))


class Links:
    def __init__(self, clock):
        self.clock = clock
        self.size = lax.axis_size("dp")
        self.bits = self.size.bit_length() - 1
        self.place = lax.axis_index("dp")
        self.core = lax.axis_index("seq")
        self.first = self.core == 0

    def bit(self, number):
        return lax.rem(lax.div(self.place, 1 << number), 2)

    def turn_bit(self, turn):
        if turn > 1:
            return self.bit(turn)
        return jnp.where(self.first, self.bit(turn), self.bit(1 - turn))

    def swap_seq(self, value):
        return lax.ppermute(value, "seq", [(0, 1), (1, 0)])

    def swap_dp(self, value, turn):
        numbers = (turn, 1 - turn if turn <= 1 else turn)
        pairs = [
            (2 * i + c, 2 * (i ^ (1 << numbers[c])) + c) for i in range(self.size) for c in range(2)
        ]
        return lax.ppermute(value, ("dp", "seq"), pairs)

    def half_places(self):
        quads = np.arange(self.size // 4, dtype=np.int32)[:, None] * 4
        near = np.arange(2, dtype=np.int32)[None, :]
        bit = self.turn_bit(0)

        def places(wanted):
            return jnp.where(
                self.first, quads + near * 2 + wanted, quads + near + wanted * 2
            ).reshape(-1)

        return jnp.stack([places(bit), places(1 - bit)])


    def scatter_first(self, value, got):
        buf, send = fold(value, got, self.clock.after(self.places))
        came = yield send, functools.partial(self.swap_dp, turn=0)
        return buf + came.astype(F32)

    def scatter_rest(self, parts, axis):
        buf = None
        for turn in range(1, self.bits):
            bit = self.turn_bit(turn)

            def cut(b):
                pieces = []
                for v in parts:
                    view = v.reshape((v.shape[0], -1, 2) + v.shape[2:])
                    pieces.append(lax.dynamic_index_in_dim(view, b, 2, keepdims=False))
                return jnp.concatenate(pieces, axis=axis) if len(pieces) > 1 else pieces[0]

            send, buf = cut(1 - bit).astype(BF), cut(bit)
            came = yield send, functools.partial(self.swap_dp, turn=turn)
            buf = buf + came.astype(F32)
            parts = [buf]
        return buf

    def sum_far(self, value):
        for turn in range(2, self.bits):
            low = value.astype(BF)
            came = yield low, functools.partial(self.swap_dp, turn=turn)
            value = low.astype(F32) + came.astype(F32)
        return value

    def order(self, bit, same, other, axis):
        return jnp.where(
            bit == 0, jnp.stack([same, other], axis=axis), jnp.stack([other, same], axis=axis)
        )

    def gather_near(self, buf, at):
        came = yield buf, functools.partial(self.swap_dp, turn=1)
        buf = self.order(self.turn_bit(1), buf, came, at)
        came = yield buf, functools.partial(self.swap_dp, turn=0)
        return jnp.where(
            self.first,
            self.order(self.bit(0), buf, came, at + 1),
            self.order(self.bit(1), buf, came, at),
        )

    def gather(self, value, axis):
        buf, at = value, axis
        for turn in range(self.bits - 1, 1, -1):
            came = yield buf, functools.partial(self.swap_dp, turn=turn)
            buf = self.order(self.bit(turn), buf, came, at)
            at += 1
        buf = yield from self.gather_near(buf, at)
        shape = value.shape
        return buf.reshape(shape[:axis] + (shape[axis] * self.size,) + shape[axis + 1 :])

    def gather_rows(self, buf):
        for turn in range(self.bits - 1, 0, -1):
            came = yield buf, functools.partial(self.swap_dp, turn=turn)
            buf = jnp.concatenate([buf, came], axis=1)
        came = yield buf, functools.partial(self.swap_dp, turn=0)
        return buf, came

    def sum_blocks(self, value):
        rows, width = value.shape
        view = value.reshape(2, 2, rows // 4, width)
        cut = lambda b: jnp.where(
            self.first,
            lax.dynamic_index_in_dim(view, b, 1, keepdims=False),
            lax.dynamic_index_in_dim(view, b, 0, keepdims=False),
        )
        bit = self.turn_bit(0)
        came = yield cut(1 - bit).astype(BF), functools.partial(self.swap_dp, turn=0)
        buf = cut(bit) + came.astype(F32)
        bit = self.turn_bit(1)
        half = lambda b: lax.dynamic_index_in_dim(buf, b, 0, keepdims=False)
        came = yield half(1 - bit).astype(BF), functools.partial(self.swap_dp, turn=1)
        buf = yield from self.sum_far(half(bit) + came.astype(F32))
        buf = yield from self.gather_near(buf.astype(BF), 0)
        return buf.reshape(rows, width)

    def all_sum(self, value):
        for turn in range(self.bits):
            came = yield value, functools.partial(self.swap_dp, turn=turn)
            value = value + came
        came = yield value, self.swap_seq
        return value + came

    def by_core(self, own, other, axis):
        return jnp.where(
            self.first,
            jnp.concatenate([own, other], axis=axis),
            jnp.concatenate([other, own], axis=axis),
        )


def held(value, other):
    where = pl.BlockSpec(memory_space=pl.ANY)
    return pl.pallas_call(
        lambda *refs: None,
        in_specs=[where, where],
        out_specs=where,
        out_shape=jax.ShapeDtypeStruct(value.shape, value.dtype),
        input_output_aliases={0: 0},
        cost_estimate=SMALL,
        name="held",
    )(value, other)


def tie(value, others):
    return lax.optimization_barrier((value, *others))[0]


class Order:
    def __init__(self):
        self.last = ()

    def after(self, value):
        return tie(value, self.last) if self.last else value

    def done(self, *values):
        self.last = values


class Chain:
    def __init__(self, order, steps):
        self.clock, self.steps, self.result = order, steps, None
        self.launch(*next(steps))

    def launch(self, send, how, free=False):
        self.flight, self.free = how(send), free
        self.clock.done(send)

    def step(self, count=1):
        for _ in range(count):
            if self.steps is None:
                return
            try:
                came = self.flight if self.free else self.clock.after(self.flight)
                self.launch(*self.steps.send(came))
            except StopIteration as end:
                self.result, self.steps = end.value, None
                self.clock.done(*jax.tree.leaves(self.result))

    def finish(self):
        while self.steps is not None:
            self.step()
        return self.result


def pack_gram(gram):
    count = gram.shape[0] // TILE
    row = lambda i: gram[i * TILE : (i + 1) * TILE, i * TILE :]
    return jnp.concatenate(
        [jnp.concatenate([row(i), row(count - 1 - i)], axis=1) for i in range(count // 2)], axis=0
    )


def unpack_gram(packed):
    count = 2 * packed.shape[0] // TILE
    blocks = {}
    for i in range(count // 2):
        strip = packed[i * TILE : (i + 1) * TILE]
        for j in range(i, count):
            blocks[i, j] = strip[:, (j - i) * TILE : (j - i + 1) * TILE]
        low = count - 1 - i
        for j in range(low, count):
            blocks[low, j] = strip[:, (count - i + j - low) * TILE : (count - i + j - low + 1) * TILE]
    rows = []
    for i in range(count):
        rows.append(
            jnp.concatenate([blocks[i, j] if j >= i else blocks[j, i].T for j in range(count)], axis=1)
        )
    return jnp.concatenate(rows, axis=0)


def muon_kernel(parts, gathered, scaling, *refs):
    sources, (mom_ref, master_ref, out_ref) = refs[:parts], refs[parts:]
    if gathered:
        whole = jnp.concatenate([ref[0] for ref in sources], axis=0)
        gram = mm(whole, whole, TN)
    else:
        gram = unpack_gram(sources[0][0].astype(F32))
    width = gram.shape[1]
    row = lax.broadcasted_iota(jnp.int32, (width, width), 0)
    column = lax.broadcasted_iota(jnp.int32, (width, width), 1)
    trace = jnp.sum(
        jnp.sum(jnp.where(row == column, gram, 0.0), axis=0, keepdims=True), axis=1, keepdims=True
    )
    scale = 1.0 / (jnp.sqrt(trace) + frob_eps)
    unit = gram * (scale * scale)
    unit_low = unit.astype(BF)
    rest_one = (coeff_b * unit + coeff_c * mm(unit_low, unit_low, NN)).astype(BF)
    cross = mm(rest_one, unit_low, NN)
    second = (
        (coeff_a * coeff_a) * unit
        + (2.0 * coeff_a) * cross
        + mm(rest_one, cross.astype(BF), NN)
    )
    second_low = second.astype(BF)
    rest_two = (coeff_b * second + coeff_c * mm(second_low, second_low, NN)).astype(BF)
    ortho = mom_ref[0] * scale
    ortho = coeff_a * ortho + mm(ortho.astype(BF), rest_one, NN)
    ortho = coeff_a * ortho + mm(ortho.astype(BF), rest_two, NN)
    out_ref[0] = master_ref[0] * (1.0 - muon_rate * muon_decay) - (muon_rate * scaling) * ortho


def gram_kernel(mom_ref, out_ref):
    low = mom_ref[...].astype(BF)
    out_ref[...] = pack_gram(mm(low, low, TN))


def packed_gram(mom):
    width = mom.shape[1]
    return pl.pallas_call(
        gram_kernel,
        out_shape=jax.ShapeDtypeStruct((width // 2, width + TILE), F32),
        compiler_params=pltpu.CompilerParams(vmem_limit_bytes=24 << 20),
        cost_estimate=SMALL,
        name="gram",
    )(mom)


def muon(sources, gathered, mom, master, scaling):
    count, rows, width = mom.shape
    one = lambda shape: pl.BlockSpec((1,) + shape, lambda m: (m, 0, 0))
    return pl.pallas_call(
        functools.partial(muon_kernel, len(sources), gathered, scaling),
        grid=(count,),
        in_specs=[one(v.shape[1:]) for v in sources] + [one((rows, width)), one((rows, width))],
        out_specs=one((rows, width)),
        out_shape=jax.ShapeDtypeStruct(mom.shape, F32),
        compiler_params=pltpu.CompilerParams(vmem_limit_bytes=48 << 20),
        cost_estimate=SMALL,
        name="muon",
    )(*sources, mom, master)


def per_device(
    hidden_in,
    out_grad,
    seg_lengths,
    attn_master,
    ffn_master,
    attn_moment,
    ffn_moment,
    gains,
    gain_first,
    gain_second,
    bias_table,
    bias_first,
    bias_second,
):
    clock = Order()
    links = Links(clock)
    row_len = hidden_in.shape[1] * lax.axis_size("seq")
    heads = bias_table.shape[1]
    core = links.core
    first = links.first
    flag = first.astype(jnp.int32).reshape(1)
    core_at = core.astype(jnp.int32).reshape(1)
    width = attn_master.shape[2]
    pairs = heads // 2
    strip = width // 2
    half = ffn_master.shape[1] // 2
    size = links.size

    def pick(value, count):
        return lax.dynamic_slice_in_dim(value, core * count, count, 0)

    ffn_own = lax.dynamic_slice_in_dim(ffn_master, core * half, half, axis=1).astype(BF)
    ffn_w = lax.all_gather(ffn_own, ("dp", "seq"), axis=1, tiled=True)

    def attn_weights(shard):
        own = yield from links.gather(shard, 1)
        other = yield own, links.swap_seq
        return own, other

    weights = Chain(
        clock,
        attn_weights(
            lax.dynamic_slice_in_dim(attn_master, core * strip, strip, axis=2).astype(BF)
        ),
    )

    def row_halves(value):
        view = value.reshape((2, value.shape[0] // 2) + value.shape[1:])
        own, send = (lax.dynamic_index_in_dim(view, c, 0, keepdims=False) for c in (core, 1 - core))
        return own, send

    hidden_own, hidden_send = row_halves(hidden_in)
    cot_own, cot_send = row_halves(out_grad)
    hidden_other = links.swap_seq(hidden_send)
    cot_other = links.swap_seq(cot_send)
    clock.done(hidden_send, cot_send)
    weights.step()

    rows = hidden_own.shape[0]
    tokens = rows * row_len
    hidden_low = links.by_core(hidden_own, clock.after(hidden_other), 1).reshape(tokens, width)
    hidden = hidden_low.astype(F32)
    scale_one = lax.rsqrt(jnp.mean(hidden * hidden, axis=-1, keepdims=True) + norm_eps)
    normed = (hidden * scale_one * gains[0]).astype(BF)
    clock.done(normed)
    weights.step()

    seg_rows = lax.dynamic_slice_in_dim(seg_lengths, core * rows, rows, 0)
    seg_ends = jnp.cumsum(seg_rows, axis=-1)
    places = jnp.arange(row_len, dtype=jnp.int32)
    seg_full = jnp.sum((places[None, :, None] >= seg_ends[:, None, :]).astype(jnp.int32), axis=-1)
    valid = (seg_full < seg_rows.shape[1]).reshape(tokens, 1)
    seg_col = seg_full.reshape(rows, row_len, 1)
    seg_row = seg_full.reshape(rows, 1, row_len)
    cot_rows = links.by_core(cot_own, clock.after(cot_other), 1).reshape(tokens, width)
    cotangent = jnp.where(valid, cot_rows, jnp.zeros((), BF))
    onehot = offset_onehot(bias_table.shape[0])
    onehot_rev = np.concatenate([onehot[-2::-1], onehot[-1:]], axis=0)
    trev = exact_dot(onehot_rev, bias_table, "mb,bh->hm").reshape(heads // 2, 2, 4 * TILE)
    links.places = links.half_places()
    clock.done(cotangent, seg_col, seg_row, trev, links.places)
    weights.step()

    moment_attn = pick(attn_moment, 2)
    w_own, w_other = weights.finish()
    proj = project(core_at, normed, w_own, w_other)
    out_w = links.by_core(w_own[3], w_other[3], 1)
    context, lse = attend(proj, trev, seg_col, seg_row, rows, row_len, 0)

    middle = hidden + mm(context, out_w, NN)
    scale_two = lax.rsqrt(jnp.mean(middle * middle, axis=-1, keepdims=True) + norm_eps)
    normed_two = (middle * scale_two * gains[1]).astype(BF)

    def ffn_first(keep, send):
        view = (1, size, half, width)
        came = yield send, links.swap_seq, True
        return (yield from links.scatter_first(keep.reshape(view), came.reshape(view)))

    def ffn_rest(first_part, second_part):
        total = yield from links.scatter_rest([first_part, second_part], 2)
        return total.reshape(1, 2 * half, width)

    y_parts, dn_parts, sums = [], [], []
    clock.done(normed_two)
    for p in range(2):
        y, dn, keep, send = ffn(clock.after(flag), normed_two, cotangent, ffn_w, size, p)
        y_parts.append(y)
        dn_parts.append(dn)
        sums.append(Chain(clock, ffn_first(keep, send)))
    one, two = sums
    one.step()
    out_own, out_send, middle_grad, context_grad, out_map_grad, gain_two_part = middle_back(
        clock.after(core_at), middle, cotangent, gains[1:2], out_w, y_parts, dn_parts, context, rows
    )
    clock.done(gain_two_part)

    done_grads, diag = [], []
    near = [0, 0]
    sizes = (pairs - pairs // 3, pairs // 3)

    def back(group, grads, count=2):
        start, member = sum(sizes[:group]), near[group]
        near[group] += count
        grads, diag_m = attend_back(
            proj,
            trev,
            seg_col,
            clock.after(seg_row),
            lse,
            context_grad,
            rows,
            row_len,
            start + member,
            member,
            count,
            sizes[group],
            grads,
        )
        diag.append(diag_m)
        clock.done(diag_m)
        return grads

    def maps(group, grads):
        done_grads.append(grads)
        keep, send = maps_grad(
            clock.after(flag), normed, grads, out_map_grad, sum(sizes[:group]) * TILE
        )
        clock.done(send)
        return keep, send

    def attn_first(group, keep, send):
        view = (2, size, width // size, sizes[group] * TILE)
        came = yield send, links.swap_seq, True
        return (yield from links.scatter_first(keep.reshape(view), came.reshape(view)))

    def attn_rest(first_group, second_group):
        total = yield from links.scatter_rest([first_group, second_group], 3)
        grad = total.reshape(2, width // size, width)
        mom = muon_beta * moment_attn + grad
        whole = yield from links.gather_rows(mom.astype(BF))
        return grad, mom, whole

    two.step()
    grads = back(0, None)
    grads = back(0, grads)
    first_part, second_part = one.finish(), two.finish()
    units = Chain(clock, ffn_rest(first_part, second_part))
    three = Chain(clock, attn_first(0, *maps(0, grads)))
    grads = back(1, None)
    three.step()
    four = Chain(clock, attn_first(1, *maps(1, grads)))
    units.step()
    four.step()
    grad_own, grad_send, gain_one_part = entry_back(
        clock.after(core_at), hidden_low, middle_grad, gains[0:1], w_own, w_other, done_grads, rows
    )
    clock.done(gain_one_part)
    first_group, second_group = three.finish(), four.finish()
    maps_sum = Chain(clock, attn_rest(first_group, second_group))
    units.step()
    out_other = links.swap_seq(clock.after(out_send))
    diag = jnp.concatenate(diag, axis=0).reshape(heads, 4 * TILE)
    table_grad = exact_dot(onehot_rev, diag, "mb,hm->bh")
    small = jnp.concatenate(
        [
            jnp.sum(gain_one_part, axis=0),
            jnp.sum(gain_two_part, axis=0),
            table_grad.reshape(-1),
        ]
    )
    small = Chain(clock, links.all_sum(small))
    maps_sum.step()
    hidden_out = links.by_core(out_own, clock.after(out_other), 0)
    clock.done(hidden_out)
    maps_sum.step()
    units.flight = held(units.flight, maps_sum.flight)
    ffn_grad = units.finish()
    mom_ffn = muon_beta * pick(ffn_moment, 1) + ffn_grad
    gram = Chain(clock, links.sum_blocks(packed_gram(mom_ffn[0])))
    small.step()
    grad_other = links.swap_seq(clock.after(grad_send))
    maps_sum.step()
    gram.step()
    small.step()
    gram.step()
    grad_tokens = links.by_core(grad_own, clock.after(grad_other), 0)
    clock.done(grad_tokens)
    maps_sum.step()
    small.step()
    gram.step()
    ffn_other = links.swap_seq(clock.after(ffn_grad))
    maps_sum.step()
    gram.step()
    ffn_mom = muon_beta * ffn_moment + links.by_core(ffn_grad, clock.after(ffn_other), 0)
    clock.done(ffn_mom)
    maps_sum.step()
    gram.step()
    small.step()
    if links.bits > 4:
        maps_sum.step(2 * links.bits - 8)
    gram_ffn, small = gram.finish(), small.finish()
    gain_sum = small[: 2 * width].reshape(2, width)
    table_sum = small[2 * width :].reshape(table_grad.shape)
    attn_grad, mom_attn, attn_whole = maps_sum.finish()
    attn_other = links.swap_seq(attn_grad)
    new_attn = muon(attn_whole, True, mom_attn, pick(attn_master, 2), 1.0)
    new_ffn = muon(
        [held(gram_ffn, new_attn)[None]],
        False,
        mom_ffn,
        pick(ffn_master, 1),
        math.sqrt(max(1.0, FF / D)),
    )
    attn_mom = muon_beta * attn_moment + links.by_core(attn_grad, attn_other, 0)
    new_gains, new_gain_first, new_gain_second = adamw(gains, gain_first, gain_second, gain_sum)
    new_bias, new_bias_first, new_bias_second = adamw(
        bias_table, bias_first, bias_second, table_sum
    )
    return (
        hidden_out,
        grad_tokens,
        new_attn,
        attn_mom,
        new_ffn,
        ffn_mom,
        new_gains,
        new_gain_first,
        new_gain_second,
        new_bias,
        new_bias_first,
        new_bias_second,
    )


def solution(mesh):
    in_specs = (
        P("dp", "seq", None),
        P("dp", "seq", None),
        P("dp", None),
        P(None, "dp", None),
        P(None, "dp", None),
        P(None, "dp", None),
        P(None, "dp", None),
        P(),
        P(),
        P(),
        P(),
        P(),
        P(),
    )
    out_specs = (
        P("dp", "seq", None),
        P("dp", "seq", None),
        P("seq", "dp", None),
        P(None, "dp", None),
        P("seq", "dp", None),
        P(None, "dp", None),
        P(),
        P(),
        P(),
        P(),
        P(),
        P(),
    )
    return jax.shard_map(
        per_device, mesh=mesh, in_specs=in_specs, out_specs=out_specs, check_vma=False
    )
```
